128 devices in a mesh: dp: 64 (over z, y, x_hi, core), mp: 2 (over x_lo).
Axes of the slice: x: 4 (x_hi: 2, x_lo: 2; x = x_hi * 2 + x_lo), y: 4, z: 4, core: 2. Of those that a mesh axis runs over, the one named last changes fastest.
Arguments:
- hidden_rows: bfloat16 [16384, 8192], P(('dp', 'mp')), may hold values from -6 to 6
- key_grads: bfloat16 [16384, 1024], P('dp', 'mp'), may hold values from -6 to 6
- loss_mask: int32 [16384], P('dp'), may hold values 0 or 1
- key_weight: bfloat16 [8192, 1024], P(None, 'mp'), may hold values from -0.1875 to 0.1875
- error_buf: bfloat16 [64, 8192, 1024], P('dp', None, 'mp'), may hold values from -6 to 6
- right_factor: float32 [1024, 64], P('mp'), may hold values from -6 to 6
Outputs:
- input_grad: bfloat16 [16384, 8192], P(('dp', 'mp'))
- update: bfloat16 [8192, 1024], P(None, 'mp')
- new_error: bfloat16 [64, 8192, 1024], P('dp', None, 'mp')
- new_factor: float32 [1024, 64], P('mp')
The draws below stay inside these ranges and needn't reach their ends.
All inputs are finite; a program needn't handle non-finite values. No bound on the sum of `loss_mask` on one device may be relied on, other than what follows from the above.
Results may differ from the reference program's by a relative error of at most 0.00115.
Values may be sent and summed in bfloat16 or wider, within the bound.
No kernel may reach another device: no remote copies, remote signals or barrier semaphores. Data moves between devices by JAX's collectives and lax.ppermute only.
A program may use at most 256 MiB of HBM per device.

```python
import jax
import jax.numpy as jnp
from jax import lax

D = 8192
KV = 1024
R = 64
TOK = 256
REPLICAS = 64
TOKENS = 16384


def place_ends(drawn, stream_key, low, largest):
    longest = drawn.shape.index(max(drawn.shape))
    spots = []
    for shift in (0, 1):
        where = [jax.random.randint(jax.random.fold_in(stream_key, axis), (), 0, length) for axis, length in enumerate(drawn.shape)]
        where[longest] = (where[longest] + shift) % drawn.shape[longest]
        spots.append(tuple(where))
    return drawn.at[spots[0]].set(low).at[spots[1]].set(largest)


def block_levels(stream_key, extent, split, least, largest):
    factor_of = 1.0
    for dim, shards_of in split:
        steps = jax.random.uniform(jax.random.fold_in(jax.random.fold_in(stream_key, 6), dim), (shards_of,), jnp.float32, least / len(split), largest / len(split))
        factor_of = factor_of * jnp.repeat(jnp.exp(steps), extent[dim] // shards_of).reshape((-1,) + (1,) * (len(extent) - 1 - dim))
    return factor_of


def noise(own_key, shape, scale, bound, split=(), dtype=jnp.bfloat16):
    drawn = jax.random.normal(own_key, shape, jnp.float32) * scale
    if len(split) > 0:
        drawn = block_levels(own_key, shape, split, -0.22, 0.18) * drawn
    return jnp.clip(drawn, min=-bound, max=bound).astype(dtype)


def setup_inputs(seed: int = 0) -> dict:
    splits = jax.random.split(jax.random.key(seed), 7)
    return {
        "hidden_rows": noise(splits[0], (TOKENS, D), 1.0, 6.0, ((0, 128),)),
        "key_grads": noise(splits[1], (TOKENS, KV), 1.0, 6.0, ((0, 64), (1, 2))),
        "loss_mask": place_ends((jax.random.randint(splits[2], (TOKENS,), 0, 4) < 3).astype(jnp.int32), jax.random.fold_in(splits[2], 1), 0, 1),
        "key_weight": noise(splits[3], (D, KV), KV ** -0.5, 0.1875, ((1, 2),)),
        "error_buf": noise(splits[4], (REPLICAS, D, KV), 1.0, 6.0, ((0, 64), (2, 2))),
        "right_factor": noise(splits[5], (KV, R), 1.0, 6.0, ((0, 2),), jnp.float32),
    }


def orthonormal(left_sum, gram_matrix):
    factor_low = jnp.linalg.cholesky(gram_matrix)
    return jax.scipy.linalg.solve_triangular(factor_low, left_sum.T, lower=True).T

def reference(hidden_rows, key_grads, loss_mask, key_weight, error_buf, right_factor):
    highest = lax.Precision.HIGHEST
    masked = key_grads * loss_mask[:, None].astype(jnp.bfloat16)
    input_grad = lax.dot_general(masked.astype(jnp.float32), key_weight.astype(jnp.float32), (((1,), (1,)), ((), ())), preferred_element_type=jnp.float32).astype(jnp.bfloat16)
    hidden_stack = hidden_rows.reshape(REPLICAS, TOK, D)
    masked_stack = masked.reshape(REPLICAS, TOK, KV)

    def gradient(running, items):
        hidden_part, masked_part, error_part = items
        weight_grad = lax.dot_general(hidden_part.astype(jnp.float32), masked_part.astype(jnp.float32), (((0,), (0,)), ((), ())), preferred_element_type=jnp.float32) * TOK ** (-0.5)
        merged = weight_grad + error_part.astype(jnp.float32)
        return (running + jnp.dot(merged, right_factor, precision=highest), merged)
    left_sum, merged_all = lax.scan(gradient, jnp.zeros((D, R), jnp.float32), (hidden_stack, masked_stack, error_buf))
    gram_matrix = jnp.dot(left_sum.T, left_sum, precision=highest)
    ortho_basis = orthonormal(left_sum, gram_matrix)

    def project(running, merged):
        return (running + jnp.dot(merged.T, ortho_basis, precision=highest), None)
    right_sum, unused = lax.scan(project, jnp.zeros((KV, R), jnp.float32), merged_all)
    new_factor = right_sum / REPLICAS
    estimate = jnp.dot(ortho_basis, new_factor.T, precision=highest)
    new_error = (merged_all - estimate[None]).astype(jnp.bfloat16)
    return (input_grad, estimate.astype(jnp.bfloat16), new_error, new_factor)
```

```python
import functools

import jax
import jax.numpy as jnp
import numpy as np
from jax import lax
from jax.experimental import pallas as pl
from jax.experimental.pallas import tpu as pltpu
from jax.sharding import Mesh
from jax.sharding import PartitionSpec as P

AXES = ("z", "y", "xh", "core", "xl")
SIZES = (4, 4, 2, 2, 2)
BF = jnp.bfloat16
F32 = jnp.float32
HIGHEST = lax.Precision.HIGHEST
BLK = 512
VMEM_LIMIT = 40 * 1024 * 1024


def permutation(z=0, y=0, x=0, core=0, flip=None):
    pairs = []
    for source in range(128):
        cz, cy, ch, cc, cl = (int(v) for v in np.unravel_index(source, SIZES))
        cx = ch * 2 + cl
        cx = (cx + x) % 4 if flip is None else flip[cx]
        target = ((cz + z) % 4, (cy + y) % 4, cx // 2, (cc + core) % 2, cx % 2)
        pairs.append((source, int(np.ravel_multi_index(target, SIZES))))
    return pairs


OTHER_CORE = permutation(core=1)
PARTNER = permutation(flip=(1, 0, 3, 2))
WRAP = permutation(flip=(3, 2, 1, 0))


def send(array, pairs):
    return lax.ppermute(array, AXES, pairs)


def sum_of_four(array, axis):
    ahead = send(array, permutation(**{axis: 1}))
    behind = send(array, permutation(**{axis: 3}))
    across = send(array, permutation(**{axis: 2}))
    return (array + across) + (ahead + behind)


def split3(value, axis):
    a = lax.reduce_precision(value, 8, 7)
    b = lax.reduce_precision(value - a, 8, 7)
    c = value - a - b
    return jnp.concatenate([a.astype(BF), b.astype(BF), c.astype(BF)], axis=axis)


def kernel_split3(value):
    a = value.astype(BF)
    rest = value - a.astype(F32)
    b = rest.astype(BF)
    c = (rest - b.astype(F32)).astype(BF)
    return a, b, c


def dot(a, b, contract):
    return lax.dot_general(a, b, ((contract[:1], contract[1:]), ((), ())), preferred_element_type=F32)


def left_kernel(core_ref, err, hid_lo, hid_hi, rfs, toks, keep, away):
    step = pl.program_id(0)
    halves = []
    for half, hid in ((0, hid_lo), (1, hid_hi)):
        wide = dot(err[half], rfs[...], (1, 0)) + dot(hid[...], toks[...], (0, 0))
        halves.append(wide[:, :64] + wide[:, 64:128] + wide[:, 128:192])
    both = jnp.concatenate(halves, axis=1)

    @pl.when(step < 4)
    def _():
        away[...] = both

    @pl.when(step >= 4)
    def _():
        keep[...] = both


def first4(i, core):
    return (jnp.minimum(i, 3), 0)


def last4(i, core):
    return (jnp.maximum(i - 4, 0), 0)


def left_part(core, err, hidden, rfs, toks):
    def block(i, c):
        return ((1 - c[0]) * 4 + i) % 8

    return pl.pallas_call(
        left_kernel,
        out_shape=(jax.ShapeDtypeStruct((2048, 128), F32), jax.ShapeDtypeStruct((2048, 128), F32)),
        grid_spec=pltpu.PrefetchScalarGridSpec(
            num_scalar_prefetch=1,
            grid=(8,),
            in_specs=[
                pl.BlockSpec((2, BLK, 512), lambda i, c: (0, block(i, c), 0)),
                pl.BlockSpec((128, BLK), lambda i, c: (0, block(i, c))),
                pl.BlockSpec((128, BLK), lambda i, c: (0, block(i, c) + 8)),
                pl.BlockSpec((512, 192), lambda i, c: (0, 0)),
                pl.BlockSpec((128, 192), lambda i, c: (0, 0)),
            ],
            out_specs=[pl.BlockSpec((BLK, 128), last4), pl.BlockSpec((BLK, 128), first4)],
        ),
        compiler_params=pltpu.CompilerParams(vmem_limit_bytes=VMEM_LIMIT),
        cost_estimate=pl.CostEstimate(flops=3 * 10**9, bytes_accessed=13 * 2**20, transcendentals=0),
        name="left_part",
    )(core, err, hidden, hidden, rfs, toks)


def right_kernel(core_ref, mine, other, err, own_lo, own_hi, oa_lo, oa_hi, ob_lo, ob_hi, masked, right, gram, z_acc, w_acc, g_acc):
    step = pl.program_id(0)

    @pl.when(step == 0)
    def _():
        z_acc[...] = jnp.zeros_like(z_acc)
        w_acc[...] = jnp.zeros_like(w_acc)
        g_acc[...] = jnp.zeros_like(g_acc)

    packed = jnp.where(step < 4, mine[...], other[...])
    for half, hids in ((0, (own_lo, oa_lo, ob_lo)), (1, (own_hi, oa_hi, ob_hi))):
        terms = jnp.concatenate(kernel_split3(packed[:, half * 64 : half * 64 + 64]), axis=1)
        rows = jnp.concatenate([h[...] for h in hids], axis=0)
        z_acc[...] += dot(rows, terms, (1, 0))
        w_acc[...] += dot(terms, err[half], (0, 0))
        g_acc[...] += dot(terms, terms, (0, 0))

    @pl.when(step == 7)
    def _():
        z = z_acc[...]
        z = (z[:, :64] + z[:, 64:128] + z[:, 128:192]) * (1.0 / 16.0)
        wide = w_acc[...] + dot(jnp.concatenate(kernel_split3(z), axis=1), masked[...], (0, 0))
        right[...] = wide[:64] + wide[64:128] + wide[128:192]
        g = g_acc[...]
        g = g[:64] + g[64:128] + g[128:192]
        gram[...] = g[:, :64] + g[:, 64:128] + g[:, 128:192]


def right_part(core, mine, other, err, own, other_a, other_b, masked):
    def block(i, c):
        return (c[0] * 4 + i) % 8

    def lo(i, c):
        return (0, block(i, c))

    def hi(i, c):
        return (0, block(i, c) + 8)

    return pl.pallas_call(
        right_kernel,
        out_shape=(jax.ShapeDtypeStruct((64, 512), F32), jax.ShapeDtypeStruct((64, 64), F32)),
        grid_spec=pltpu.PrefetchScalarGridSpec(
            num_scalar_prefetch=1,
            grid=(8,),
            in_specs=[
                pl.BlockSpec((BLK, 128), first4),
                pl.BlockSpec((BLK, 128), last4),
                pl.BlockSpec((2, BLK, 512), lambda i, c: (0, block(i, c), 0)),
                pl.BlockSpec((128, BLK), lo),
                pl.BlockSpec((128, BLK), hi),
                pl.BlockSpec((64, BLK), lo),
                pl.BlockSpec((64, BLK), hi),
                pl.BlockSpec((64, BLK), lo),
                pl.BlockSpec((64, BLK), hi),
                pl.BlockSpec((256, 512), lambda i, c: (0, 0)),
            ],
            out_specs=[pl.BlockSpec((64, 512), lambda i, c: (0, 0)), pl.BlockSpec((64, 64), lambda i, c: (0, 0))],
            scratch_shapes=[pltpu.VMEM((256, 192), F32), pltpu.VMEM((192, 512), F32), pltpu.VMEM((192, 192), F32)],
        ),
        compiler_params=pltpu.CompilerParams(vmem_limit_bytes=VMEM_LIMIT),
        cost_estimate=pl.CostEstimate(flops=4 * 10**9, bytes_accessed=14 * 2**20, transcendentals=0),
        name="right_part",
    )(core, mine, other, err, own, own, other_a, other_a, other_b, other_b, masked)


def final_kernel(core_ref, mine, other, err, own_lo, own_hi, oa_lo, oa_hi, ob_lo, ob_hi, masked, factor, update, new_error):
    step = pl.program_id(0)
    packed = jnp.where(step < 4, mine[...], other[...])
    n1 = factor[...].astype(BF)
    n2 = (factor[...] - n1.astype(F32)).astype(BF)
    factors = jnp.concatenate([n1, n2, n1], axis=0)
    for half, hids in ((0, (own_lo, oa_lo, ob_lo)), (1, (own_hi, oa_hi, ob_hi))):
        basis = packed[:, half * 64 : half * 64 + 64]
        o1 = basis.astype(BF)
        o2 = (basis - o1.astype(F32)).astype(BF)
        estimate = dot(jnp.concatenate([o1, o1, o2], axis=1), factors, (1, 0))
        rows = jnp.concatenate([h[...] for h in hids], axis=0)
        merged = dot(rows, masked[...], (0, 0)) * (1.0 / 16.0) + err[half].astype(F32)
        update[half] = estimate.astype(BF)
        new_error[half] = (merged - estimate).astype(BF)


def final_part(core, mine, other, err, own, other_a, other_b, masked, factor):
    def block(i, c):
        return (c[0] * 4 + i) % 8

    def lo(i, c):
        return (0, block(i, c))

    def hi(i, c):
        return (0, block(i, c) + 8)

    def rows(i, c):
        return (0, block(i, c), 0)

    return pl.pallas_call(
        final_kernel,
        out_shape=(jax.ShapeDtypeStruct((2, 4096, 512), BF), jax.ShapeDtypeStruct((2, 4096, 512), BF)),
        grid_spec=pltpu.PrefetchScalarGridSpec(
            num_scalar_prefetch=1,
            grid=(8,),
            in_specs=[
                pl.BlockSpec((BLK, 128), first4),
                pl.BlockSpec((BLK, 128), last4),
                pl.BlockSpec((2, BLK, 512), rows),
                pl.BlockSpec((128, BLK), lo),
                pl.BlockSpec((128, BLK), hi),
                pl.BlockSpec((64, BLK), lo),
                pl.BlockSpec((64, BLK), hi),
                pl.BlockSpec((64, BLK), lo),
                pl.BlockSpec((64, BLK), hi),
                pl.BlockSpec((256, 512), lambda i, c: (0, 0)),
                pl.BlockSpec((64, 512), lambda i, c: (0, 0)),
            ],
            out_specs=[pl.BlockSpec((2, BLK, 512), rows), pl.BlockSpec((2, BLK, 512), rows)],
        ),
        compiler_params=pltpu.CompilerParams(vmem_limit_bytes=VMEM_LIMIT),
        cost_estimate=pl.CostEstimate(flops=4 * 10**9, bytes_accessed=30 * 2**20, transcendentals=0),
        name="final_part",
    )(core, mine, other, err, own, own, other_a, other_a, other_b, other_b, masked, factor)


def input_kernel(place_ref, near, far, weight_near, weight_far, out_own, out_other):
    value = dot(near[...], weight_near[...], (1, 1)) + dot(far[...], weight_far[...], (1, 1))
    value = value.astype(BF)
    out_own[...] = value[:128]
    out_other[...] = value[128:]


def input_part(place, near, far, key_weight, weight_far):
    size = weight_far.shape[0]
    steps = size // BLK
    out = jax.ShapeDtypeStruct((128, size), BF)
    return pl.pallas_call(
        input_kernel,
        out_shape=(out, out),
        grid_spec=pltpu.PrefetchScalarGridSpec(
            num_scalar_prefetch=1,
            grid=(steps,),
            in_specs=[
                pl.BlockSpec((256, 512), lambda i, p: (0, 0)),
                pl.BlockSpec((256, 512), lambda i, p: (0, 0)),
                pl.BlockSpec((BLK, 512), lambda i, p: (p[0] + i, 0)),
                pl.BlockSpec((BLK, 512), lambda i, p: (i, 0)),
            ],
            out_specs=[pl.BlockSpec((128, BLK), lambda i, p: (0, i))] * 2,
        ),
        compiler_params=pltpu.CompilerParams(vmem_limit_bytes=VMEM_LIMIT),
        cost_estimate=pl.CostEstimate(flops=size * 524288, bytes_accessed=size * 2560, transcendentals=0),
        name="input_part",
    )(place, near, far, key_weight, weight_far)


def local(hidden_rows, key_grads, loss_mask, key_weight, error_buf, right_factor):
    core = lax.axis_index("core")
    xl = lax.axis_index("xl")
    core_arg = core.astype(jnp.int32)[None]
    err = error_buf.reshape(2, 4096, 512)

    masked = key_grads * loss_mask[:, None].astype(BF)
    masked_own = lax.dynamic_slice(masked, (xl * 128, 0), (128, 512))
    masked_other = lax.dynamic_slice(masked, ((1 - xl) * 128, 0), (128, 512))
    rfs = split3(right_factor, 1)
    wide_own = dot(masked_own, rfs, (1, 0))
    wide_other = dot(masked_other, rfs, (1, 0))
    tok_own = wide_own[:, :64] + wide_own[:, 64:128] + wide_own[:, 128:]
    tok_other = wide_other[:, :64] + wide_other[:, 64:128] + wide_other[:, 128:]
    tok = (tok_own + send(tok_other, PARTNER)) * (1.0 / 16.0)
    masked_far = send(masked_other, PARTNER)

    weight_half = lax.dynamic_slice(key_weight, (core * 4096, 0), (4096, 512))
    hidden_a, hidden_b = hidden_rows[:64], hidden_rows[64:]
    hidden_a, tok = lax.optimization_barrier((hidden_a, tok))
    far_hidden_a = send(hidden_a, PARTNER)
    far_weight = [send(weight_half[:1024], WRAP)]

    keep, away = left_part(core_arg, err, hidden_rows, rfs, split3(tok, 1))
    piece = keep + send(away, OTHER_CORE)
    piece = lax.all_to_all(piece.reshape(16, 128, 128), ("z", "y"), 0, 0, tiled=True)
    piece = jnp.sum(piece, axis=0)
    piece = sum_of_four(piece, "x")

    hidden_b, weight_b, weight_c, weight_d, piece = lax.optimization_barrier(
        (hidden_b, weight_half[1024:2048], weight_half[2048:3072], weight_half[3072:], piece)
    )
    far_hidden_b = send(hidden_b, PARTNER)
    far_weight += [send(weight_b, WRAP), send(weight_c, WRAP), send(weight_d, PARTNER)]

    mine = lax.all_to_all(jnp.broadcast_to(piece[None], (16, 128, 128)), ("z", "y"), 0, 0, tiled=True)
    mine = mine.reshape(2048, 128)
    other = send(mine, OTHER_CORE)

    masked_both = jnp.concatenate([masked_own, masked_other], axis=0)
    right, gram = right_part(core_arg, mine, other, err, hidden_rows, far_hidden_a, far_hidden_b, masked_both)
    keep = lax.dynamic_slice(right, (core * 32, 0), (32, 512))
    away = lax.dynamic_slice(right, ((1 - core) * 32, 0), (32, 512))
    total = keep + send(away, OTHER_CORE)
    total = sum_of_four(total, "y")
    total = sum_of_four(total, "z")
    total = total + send(total, permutation(x=2))
    total_other = send(total, OTHER_CORE)
    right = jnp.where(core == 0, jnp.concatenate([total, total_other]), jnp.concatenate([total_other, total]))

    factor_low = jnp.linalg.cholesky(gram)
    inverse = jax.scipy.linalg.solve_triangular(factor_low, jnp.eye(64, dtype=F32), lower=True)
    empty = jnp.zeros((64, 64), F32)
    twice = jnp.concatenate([jnp.concatenate([inverse.T, empty], 1), jnp.concatenate([empty, inverse.T], 1)], 0)
    basis_mine = jnp.dot(mine, twice, precision=HIGHEST)
    basis_other = jnp.dot(other, twice, precision=HIGHEST)

    tokens_here = jnp.stack([masked_own, masked_far])
    tokens_there = send(tokens_here, OTHER_CORE)
    near = jnp.concatenate([tokens_here[0], tokens_there[0]], axis=0)
    far = jnp.concatenate([tokens_here[1], tokens_there[1]], axis=0)
    grads_own, grads_other = [], []
    for number, weight_far in enumerate(far_weight):
        place = core_arg * 8 + number * 2
        grad_own, grad_other = input_part(place, near, far, key_weight, weight_far)
        grads_own.append(grad_own)
        grads_other.append(send(grad_other, OTHER_CORE))
    input_grad = jnp.where(
        core == 0,
        jnp.concatenate(grads_own + grads_other, axis=1),
        jnp.concatenate(grads_other + grads_own, axis=1),
    )

    factor = jnp.dot(inverse, right, precision=HIGHEST) * (1.0 / 64.0)
    update, new_error = final_part(
        core_arg, basis_mine, basis_other, err, hidden_rows, far_hidden_a, far_hidden_b, masked_both, factor
    )
    return input_grad, update.reshape(8192, 512), new_error.reshape(1, 8192, 512), factor.T


def solution(mesh):
    fine = Mesh(mesh.devices.reshape(SIZES), AXES)
    dp = ("z", "y", "xh", "core")
    placed = (
        P(AXES, None),
        P(dp, "xl"),
        P(dp),
        P(None, "xl"),
        P(dp, None, "xl"),
        P("xl", None),
    )
    return jax.shard_map(
        local,
        mesh=fine,
        in_specs=placed,
        out_specs=(P(AXES, None), P(None, "xl"), P(dp, None, "xl"), P("xl", None)),
        check_vma=False,
    )
```

```python
import functools

import jax
import jax.numpy as jnp
import numpy as np
from jax import lax
from jax.experimental import pallas as pl
from jax.experimental.pallas import tpu as pltpu
from jax.sharding import Mesh
from jax.sharding import PartitionSpec as P

AXES = ("z", "y", "xh", "core", "xl")
SIZES = (4, 4, 2, 2, 2)
BF = jnp.bfloat16
F32 = jnp.float32
HIGHEST = lax.Precision.HIGHEST
BLK = 512
AHEAD = 4
SLOTS = 16
COUNT = 8192 // BLK
HALF = COUNT // 2


def permutation(z=0, y=0, x=0, core=0, flip=None):
    pairs = []
    for source in range(128):
        cz, cy, ch, cc, cl = (int(v) for v in np.unravel_index(source, SIZES))
        cx = ch * 2 + cl
        cx = (cx + x) % 4 if flip is None else flip[cx]
        target = ((cz + z) % 4, (cy + y) % 4, cx // 2, (cc + core) % 2, cx % 2)
        pairs.append((source, int(np.ravel_multi_index(target, SIZES))))
    return pairs


OTHER_CORE = permutation(core=1)
PARTNER = permutation(flip=(1, 0, 3, 2))
WRAP = permutation(flip=(3, 2, 1, 0))


def send(array, pairs):
    return lax.ppermute(array, AXES, pairs)


def sum_of_four(array, axis):
    ahead = send(array, permutation(**{axis: 1}))
    behind = send(array, permutation(**{axis: 3}))
    across = send(array, permutation(**{axis: 2}))
    return (array + across) + (ahead + behind)


def kernel_split3(value):
    a = value.astype(BF)
    rest = value - a.astype(F32)
    b = rest.astype(BF)
    c = (rest - b.astype(F32)).astype(BF)
    return a, b, c


def stack3(value):
    return jnp.concatenate(kernel_split3(value), axis=0)


def sum3(value):
    return value[:64] + value[64:128] + value[128:192]


def dot(a, b, contract):
    return lax.dot_general(a, b, ((contract[:1], contract[1:]), ((), ())), preferred_element_type=F32)


def start(copies):
    for copy in copies:
        copy.start()


def wait(copies):
    for copy in copies:
        copy.wait()


def call(kernel, name, operands, outs, scratch, limit, aliases=None, hbm=False):
    anywhere = pl.BlockSpec(memory_space=pl.ANY)
    far = [pltpu.with_memory_space_constraint(array, pltpu.HBM) for array in operands[1:]]
    return pl.pallas_call(
        kernel,
        out_shape=[(pltpu.HBM if hbm else jax.ShapeDtypeStruct)(shape, dtype) for shape, dtype in outs],
        in_specs=[pl.BlockSpec(memory_space=pltpu.SMEM)] + [pl.BlockSpec(memory_space=pltpu.HBM)] * len(far),
        out_specs=[anywhere] * len(outs),
        scratch_shapes=scratch,
        input_output_aliases=aliases or {},
        compiler_params=pltpu.CompilerParams(vmem_limit_bytes=limit * 2**20),
        cost_estimate=pl.CostEstimate(flops=1024, bytes_accessed=1024, transcendentals=0),
        name=name,
    )(operands[0], *far)


def rows_of(block):
    return pl.ds(pl.multiple_of(block * BLK, BLK), BLK)


def error_loads(err, v_err, sems, places):
    return [pltpu.make_async_copy(err.at[rows_of(p), :], v_err.at[p], sems.at[j]) for j, p in enumerate(places)]


class Group:
    def __init__(self, copies):
        self.copies = copies

    def start(self):
        start(self.copies)

    def wait(self):
        wait(self.copies)


def hidden_loads(hidden, v_hid, sems, places):
    groups = []
    for j, place in enumerate(places):
        copies, row = [], 0
        for number, part in enumerate(hidden):
            size = part.shape[0]
            copies.append(
                pltpu.make_async_copy(part.at[:, rows_of(place)], v_hid.at[place, pl.ds(row, size), :], sems.at[j, number])
            )
            row += size
        groups.append(Group(copies))
    return groups


def factor_loads(mine, other, v_left, sems, places):
    return [
        pltpu.make_async_copy((mine, other)[j // HALF].at[pl.ds(2 * (j % HALF), 2)], v_left.at[p], sems.at[j])
        for j, p in enumerate(places)
    ]


def token_kernel(
    xl_ref, grads, mask, factor_t, own, other, tok_own, tok_other, terms_t, v_grads, v_mask, v_factor, v_tok, v_masked, v_terms, sems
):
    loads = [
        pltpu.make_async_copy(grads, v_grads, sems.at[0]),
        pltpu.make_async_copy(mask, v_mask, sems.at[1]),
        pltpu.make_async_copy(factor_t, v_factor, sems.at[2]),
    ]
    start(loads)
    wait(loads)
    flags = jnp.broadcast_to(v_mask[...].astype(F32), (128, 256)).T[:, :1]
    masked = (v_grads[...].astype(F32) * flags).astype(BF)
    terms = stack3(v_factor[...])
    tok = sum3(dot(terms, masked, (1, 1))) * (1.0 / 16.0)
    first = xl_ref[0] == 0
    v_tok[0] = jnp.where(first, tok[:, 128:], tok[:, :128])
    v_tok[1] = jnp.where(first, tok[:, :128], tok[:, 128:])
    v_terms[...] = terms
    v_masked[0] = jnp.where(first, masked[:128], masked[128:])
    v_masked[1] = jnp.where(first, masked[128:], masked[:128])
    stores = [
        pltpu.make_async_copy(v_tok.at[0], tok_other, sems.at[3]),
        pltpu.make_async_copy(v_tok.at[1], tok_own, sems.at[4]),
        pltpu.make_async_copy(v_terms, terms_t, sems.at[5]),
        pltpu.make_async_copy(v_masked.at[0], own, sems.at[6]),
        pltpu.make_async_copy(v_masked.at[1], other, sems.at[7]),
    ]
    start(stores)
    wait(stores)


def token_part(xl, grads, mask, factor_t):
    return call(
        token_kernel,
        "token_part",
        (xl, grads, mask, factor_t),
        [((128, 512), BF), ((128, 512), BF), ((64, 128), F32), ((64, 128), F32), ((192, 512), BF)],
        [
            pltpu.VMEM((256, 512), BF),
            pltpu.VMEM((1, 256), jnp.int32),
            pltpu.VMEM((64, 512), F32),
            pltpu.VMEM((2, 64, 128), F32),
            pltpu.VMEM((2, 128, 512), BF),
            pltpu.VMEM((192, 512), BF),
            pltpu.SemaphoreType.DMA((8,)),
        ],
        8,
        hbm=True,
    )


def parcel_kernel(firsts, core_ref, after, hidden, key_weight, *refs):
    count = len(firsts)
    parcels, v_parcels, sems = refs[:count], refs[count : 2 * count], refs[2 * count]
    picks, drops = [], []
    for k, (kind, first) in enumerate(firsts):
        rows = parcels[k].shape[0]
        if kind == "hidden":
            source = hidden.at[pl.ds(first, rows), :]
        else:
            source = key_weight.at[pl.ds(pl.multiple_of(core_ref[0] * 4096 + first, 64), rows), :]
        picks.append(pltpu.make_async_copy(source, v_parcels[k], sems.at[0, k]))
        drops.append(pltpu.make_async_copy(v_parcels[k], parcels[k], sems.at[1, k]))
    start(picks)
    for pick, drop in zip(picks, drops):
        pick.wait()
        drop.start()
    wait(drops)


def parcel_part(core, after, hidden, key_weight, parcels):
    shapes = [((rows, 8192 if kind == "hidden" else 512), BF) for kind, _, rows in parcels]
    return call(
        functools.partial(parcel_kernel, [(kind, first) for kind, first, _ in parcels]),
        "parcel_part",
        (core, after, hidden, key_weight),
        shapes,
        [*[pltpu.VMEM(shape, dtype) for shape, dtype in shapes], pltpu.SemaphoreType.DMA((2, len(shapes)))],
        10,
        hbm=True,
    )


def left_kernel(
    core_ref, err, hidden, terms_t, tok_own, tok_far, keep, away, v_err, v_hid, v_terms, v_tok, v_out, sems, sem_err, sem_hid, sem_out
):
    small = [
        pltpu.make_async_copy(terms_t, v_terms, sems.at[0]),
        pltpu.make_async_copy(tok_own, v_tok.at[0], sems.at[1]),
        pltpu.make_async_copy(tok_far, v_tok.at[1], sems.at[2]),
    ]
    places = [(1 - core_ref[0]) * HALF + j if j < HALF else core_ref[0] * HALF + j - HALF for j in range(COUNT)]
    loads = list(zip(error_loads(err, v_err, sem_err, places), hidden_loads([hidden], v_hid, sem_hid, places)))
    start(small)
    for j in range(AHEAD):
        start(loads[j])
    wait(small)
    toks = stack3(v_tok[0] + v_tok[1])
    stores = []
    for j in range(COUNT):
        wait(loads[j])
        if j + AHEAD < COUNT:
            start(loads[j + AHEAD])
        value = sum3(dot(v_terms[...], v_err[places[j]], (1, 1)) + dot(toks, v_hid[places[j]], (1, 0)))
        v_out[j, 0] = value[:, :256]
        v_out[j, 1] = value[:, 256:]
        target = away if j < HALF else keep
        stores.append(pltpu.make_async_copy(v_out.at[j], target.at[pl.ds(2 * (j % HALF), 2)], sem_out.at[j]))
        stores[j].start()
    wait(stores)


def left_part(core, err, hidden, terms_t, tok_own, tok_far):
    return call(
        left_kernel,
        "left_part",
        (core, err, hidden, terms_t, tok_own, tok_far),
        [((16, 64, 256), F32), ((16, 64, 256), F32)],
        [
            pltpu.VMEM((COUNT, BLK, 512), BF),
            pltpu.VMEM((COUNT, 128, BLK), BF),
            pltpu.VMEM((192, 512), BF),
            pltpu.VMEM((2, 64, 128), F32),
            pltpu.VMEM((COUNT, 2, 64, 256), F32),
            pltpu.SemaphoreType.DMA((3,)),
            pltpu.SemaphoreType.DMA((COUNT,)),
            pltpu.SemaphoreType.DMA((COUNT, 1)),
            pltpu.SemaphoreType.DMA((COUNT,)),
        ],
        28,
    )


def right_kernel(count, core_ref, mine, other, err, masked_own, masked_other, *refs):
    hidden = refs[:count]
    keep, away, gram, v_left, v_err, v_hid = refs[count : count + 6]
    v_masked, v_keep, v_away, v_gram, sems, sem_left, sem_err, sem_hid = refs[count + 6 :]
    places = [core_ref[0] * HALF + j if j < HALF else (1 - core_ref[0]) * HALF + j - HALF for j in range(COUNT)]
    loads = list(
        zip(
            factor_loads(mine, other, v_left, sem_left, places),
            error_loads(err, v_err, sem_err, places),
            hidden_loads(hidden, v_hid, sem_hid, places),
        )
    )
    late = [
        pltpu.make_async_copy(masked_own, v_masked.at[pl.ds(0, 128), :], sems.at[0]),
        pltpu.make_async_copy(masked_other, v_masked.at[pl.ds(128, 128), :], sems.at[4]),
    ]
    for j in range(AHEAD):
        start(loads[j])
    start(late)
    w_sum, g_sum, z_sum = 0.0, 0.0, 0.0
    for j in range(COUNT):
        wait(loads[j])
        if j + AHEAD < COUNT:
            start(loads[j + AHEAD])
        terms = stack3(jnp.concatenate([v_left[places[j], 0], v_left[places[j], 1]], axis=1))
        w_sum = w_sum + dot(terms, v_err[places[j]], (1, 0))
        g_sum = g_sum + dot(terms, terms, (1, 1))
        z_sum = z_sum + dot(terms, v_hid[places[j]], (1, 1))
    wait(late)
    z = sum3(z_sum) * (1.0 / 16.0)
    right = sum3(w_sum + dot(stack3(z), v_masked[...], (1, 0)))
    first = core_ref[0] == 0
    v_keep[...] = jnp.where(first, right[:32], right[32:])
    v_away[...] = jnp.where(first, right[32:], right[:32])
    g = sum3(g_sum)
    v_gram[...] = g[:, :64] + g[:, 64:128] + g[:, 128:192]
    stores = [
        pltpu.make_async_copy(v_away, away, sems.at[1]),
        pltpu.make_async_copy(v_keep, keep, sems.at[2]),
        pltpu.make_async_copy(v_gram, gram, sems.at[3]),
    ]
    start(stores)
    wait(stores)


def right_part(core, mine, other, err, hidden, masked_own, masked_other):
    return call(
        functools.partial(right_kernel, len(hidden)),
        "right_part",
        (core, mine, other, err, masked_own, masked_other, *hidden),
        [((32, 512), F32), ((32, 512), F32), ((64, 64), F32)],
        [
            pltpu.VMEM((COUNT, 2, 64, 256), F32),
            pltpu.VMEM((COUNT, BLK, 512), BF),
            pltpu.VMEM((COUNT, 256, BLK), BF),
            pltpu.VMEM((256, 512), BF),
            pltpu.VMEM((32, 512), F32),
            pltpu.VMEM((32, 512), F32),
            pltpu.VMEM((64, 64), F32),
            pltpu.SemaphoreType.DMA((5,)),
            pltpu.SemaphoreType.DMA((COUNT,)),
            pltpu.SemaphoreType.DMA((COUNT,)),
            pltpu.SemaphoreType.DMA((COUNT, len(hidden))),
        ],
        28,
    )


def final_kernel(
    count, core_ref, masked_own, masked_other, total, total_other, inverse, grad_far, grad_base, mine, other, err, *refs
):
    hidden, refs = refs[:count], refs[count:]
    update, new_error, factor, grad = refs[:4]
    v_left, v_err, v_hid, v_masked, v_right, v_inv, v_factor, v_update, v_new, v_grad = refs[4:14]
    sems, sem_left, sem_err, sem_hid, sem_out = refs[14:]
    core = core_ref[0]
    places = [core * HALF + j if j < HALF else (1 - core) * HALF + j - HALF for j in range(COUNT)]
    loads = list(
        zip(
            factor_loads(mine, other, v_left, sem_left, places),
            error_loads(err, v_err, sem_err, places),
            hidden_loads(hidden, v_hid, sem_hid, places),
        )
    )
    small = [
        pltpu.make_async_copy(inverse, v_inv, sems.at[0]),
        pltpu.make_async_copy(total, v_right.at[pl.ds(pl.multiple_of(core * 32, 32), 32), :], sems.at[1]),
        pltpu.make_async_copy(total_other, v_right.at[pl.ds(pl.multiple_of((1 - core) * 32, 32), 32), :], sems.at[2]),
        pltpu.make_async_copy(masked_own, v_masked.at[pl.ds(0, 128), :], sems.at[3]),
        pltpu.make_async_copy(masked_other, v_masked.at[pl.ds(128, 128), :], sems.at[7]),
    ]
    grad_in = pltpu.make_async_copy(grad_far, v_grad, sems.at[4])
    start(small)
    for j in range(AHEAD):
        start(loads[j])
    wait(small)
    v_factor[...] = jnp.dot(v_inv[...], v_right[...], precision=HIGHEST, preferred_element_type=F32) * (1.0 / 64.0)
    coefficients = lax.dot_general(
        v_inv[...], v_factor[...], (((0,), (0,)), ((), ())), precision=HIGHEST, preferred_element_type=F32
    )
    y1, y2, y3 = kernel_split3(coefficients)
    ys = jnp.concatenate([y1, y1, y1, y2, y2, y3], axis=0)
    stores = [pltpu.make_async_copy(v_factor, factor, sems.at[5])]
    stores[0].start()
    for j in range(COUNT):
        place = places[j]
        wait(loads[j])
        if j + AHEAD < COUNT:
            start(loads[j + AHEAD])
        elif j + AHEAD == COUNT:
            grad_in.start()
        l1, l2, l3 = kernel_split3(jnp.concatenate([v_left[place, 0], v_left[place, 1]], axis=1))
        estimate = dot(jnp.concatenate([l1, l2, l3, l1, l2, l1], axis=0), ys, (0, 0))
        merged = dot(v_hid[place], v_masked[...], (0, 0)) * (1.0 / 16.0) + v_err[place].astype(F32)
        slot = j % SLOTS
        if j >= SLOTS:
            wait(stores[2 * (j - SLOTS) + 1 : 2 * (j - SLOTS) + 3])
        v_update[slot] = estimate.astype(BF)
        v_new[slot] = (merged - estimate).astype(BF)
        for k, (source, target) in enumerate(((v_update, update), (v_new, new_error))):
            copy = pltpu.make_async_copy(source.at[slot], target.at[rows_of(place), :], sem_out.at[k, slot])
            copy.start()
            stores.append(copy)
    grad_in.wait()
    columns = pl.ds(pl.multiple_of((1 - core) * 4096, 4096), 4096)
    stores.append(pltpu.make_async_copy(v_grad, grad.at[:, columns], sems.at[6]))
    stores[-1].start()
    wait(stores[:1] + stores[2 * (COUNT - SLOTS) + 1 :])


def final_part(core, masked_own, masked_other, total, total_other, inverse, grad_far, grad_base, mine, other, err, hidden):
    return call(
        functools.partial(final_kernel, len(hidden)),
        "final_part",
        (core, masked_own, masked_other, total, total_other, inverse, grad_far, grad_base, mine, other, err, *hidden),
        [((8192, 512), BF), ((8192, 512), BF), ((64, 512), F32), ((128, 8192), BF)],
        [
            pltpu.VMEM((COUNT, 2, 64, 256), F32),
            pltpu.VMEM((COUNT, BLK, 512), BF),
            pltpu.VMEM((COUNT, 256, BLK), BF),
            pltpu.VMEM((256, 512), BF),
            pltpu.VMEM((64, 512), F32),
            pltpu.VMEM((64, 64), F32),
            pltpu.VMEM((64, 512), F32),
            pltpu.VMEM((SLOTS, BLK, 512), BF),
            pltpu.VMEM((SLOTS, BLK, 512), BF),
            pltpu.VMEM((128, 4096), BF),
            pltpu.SemaphoreType.DMA((8,)),
            pltpu.SemaphoreType.DMA((COUNT,)),
            pltpu.SemaphoreType.DMA((COUNT,)),
            pltpu.SemaphoreType.DMA((COUNT, len(hidden))),
            pltpu.SemaphoreType.DMA((2, SLOTS)),
        ],
        44,
        aliases={7: 3},
    )


def input_kernel(count, core_ref, near_own, near_other, far_own, far_other, key_weight, *refs):
    pieces = refs[:count]
    grad, grad_other, v_near, v_far, v_wnear, v_wfar, v_own, v_other, sems, sem_near, sem_far, sem_out = refs[count:]
    core = core_ref[0]
    small = [
        pltpu.make_async_copy(near_own, v_near.at[pl.ds(0, 128), :], sems.at[0]),
        pltpu.make_async_copy(near_other, v_near.at[pl.ds(128, 128), :], sems.at[1]),
        pltpu.make_async_copy(far_own, v_far.at[pl.ds(0, 128), :], sems.at[2]),
        pltpu.make_async_copy(far_other, v_far.at[pl.ds(128, 128), :], sems.at[3]),
    ]
    loads, fars, ends, row = [], [], [], 0
    for j in range(4):
        place = pl.ds(pl.multiple_of(core * 4096 + j * 1024, 1024), 1024)
        loads.append(pltpu.make_async_copy(key_weight.at[place, :], v_wnear.at[j], sem_near.at[j]))
    for number, piece in enumerate(pieces):
        size = piece.shape[0]
        fars.append(pltpu.make_async_copy(piece, v_wfar.at[pl.ds(row, size), :], sem_far.at[number]))
        row += size
        ends.append(row)
    start(small)
    begun = 0
    for j in range(4):
        loads[j].start()
        while begun < count and (0 if begun == 0 else ends[begun - 1]) < (j + 1) * 1024:
            fars[begun].start()
            begun += 1
    wait(small)
    stores, waited = [], 0
    for j in range(4):
        loads[j].wait()
        while waited < count and (0 if waited == 0 else ends[waited - 1]) < (j + 1) * 1024:
            fars[waited].wait()
            waited += 1
        value = dot(v_near[...], v_wnear[j], (1, 1))
        value = (value + dot(v_far[...], v_wfar[pl.ds(j * 1024, 1024), :], (1, 1))).astype(BF)
        v_own[j] = value[:128]
        v_other[j] = value[128:]
        place = pl.ds(pl.multiple_of(core * 4096 + j * 1024, 1024), 1024)
        stores.append(pltpu.make_async_copy(v_own.at[j], grad.at[:, place], sem_out.at[0, j]))
        stores.append(pltpu.make_async_copy(v_other.at[j], grad_other.at[:, pl.ds(j * 1024, 1024)], sem_out.at[1, j]))
        start(stores[-2:])
    wait(stores)


def input_part(core, near_own, near_other, far_own, far_other, key_weight, pieces):
    return call(
        functools.partial(input_kernel, len(pieces)),
        "input_part",
        (core, near_own, near_other, far_own, far_other, key_weight, *pieces),
        [((128, 8192), BF), ((128, 4096), BF)],
        [
            pltpu.VMEM((256, 512), BF),
            pltpu.VMEM((256, 512), BF),
            pltpu.VMEM((4, 1024, 512), BF),
            pltpu.VMEM((4096, 512), BF),
            pltpu.VMEM((4, 128, 1024), BF),
            pltpu.VMEM((4, 128, 1024), BF),
            pltpu.SemaphoreType.DMA((4,)),
            pltpu.SemaphoreType.DMA((4,)),
            pltpu.SemaphoreType.DMA((len(pieces),)),
            pltpu.SemaphoreType.DMA((2, 4)),
        ],
        18,
    )


def local(hidden_rows, key_grads, loss_mask, key_weight, error_buf, right_factor):
    core = lax.axis_index("core")
    core_arg = core.astype(jnp.int32)[None]
    xl_arg = lax.axis_index("xl").astype(jnp.int32)[None]
    err = error_buf.reshape(8192, 512)
    barrier = lax.optimization_barrier

    def weight_rows(first, rows):
        return lax.dynamic_slice(key_weight, (core * 4096 + first, 0), (rows, 512))

    masked_own, masked_other, tok_own, tok_other, terms_t = token_part(
        xl_arg, key_grads, loss_mask.reshape(1, 256), right_factor.T
    )

    tok_far = send(tok_other, PARTNER)

    hidden_0, weight_0, hidden_1, weight_1, hidden_2, weight_2, weight_3, weight_4 = parcel_part(
        core_arg,
        masked_own,
        hidden_rows,
        key_weight,
        [
            ("hidden", 0, 48),
            ("weight", 0, 576),
            ("hidden", 48, 48),
            ("weight", 576, 768),
            ("hidden", 96, 32),
            ("weight", 1344, 512),
            ("weight", 1856, 1152),
            ("weight", 3008, 1088),
        ],
    )
    tok_far, hidden_0 = barrier((tok_far, hidden_0))
    far_hidden_0 = send(hidden_0, PARTNER)
    far_weight_0 = send(weight_0, WRAP)

    keep, away = left_part(core_arg, err, hidden_rows, terms_t, tok_own, tok_far)
    keep, away, far_hidden_0, far_weight_0, hidden_1, weight_1, masked_own, masked_other = barrier(
        (keep, away, far_hidden_0, far_weight_0, hidden_1, weight_1, masked_own, masked_other)
    )
    piece = keep + send(away, OTHER_CORE)
    masked_far = send(masked_other, PARTNER)
    far_hidden_1 = send(hidden_1, PARTNER)
    far_weight_1 = send(weight_1, WRAP)
    piece = lax.all_to_all(piece, ("z", "y"), 0, 0, tiled=True)
    piece = jnp.sum(piece, axis=0)
    piece, far_hidden_1, far_weight_1, masked_far = barrier((piece, far_hidden_1, far_weight_1, masked_far))
    piece = sum_of_four(piece, "x")

    piece, hidden_2, weight_2, masked_own, masked_far = barrier((piece, hidden_2, weight_2, masked_own, masked_far))
    far_hidden_2 = send(hidden_2, PARTNER)
    far_weight_2 = send(weight_2, WRAP)
    near_other = send(masked_own, OTHER_CORE)
    far_other = send(masked_far, OTHER_CORE)
    mine = lax.all_to_all(jnp.broadcast_to(piece[None], (16, 64, 256)), ("z", "y"), 0, 0, tiled=True)
    mine, far_hidden_2, far_weight_2, weight_3, weight_4, near_other, far_other = barrier(
        (mine, far_hidden_2, far_weight_2, weight_3, weight_4, near_other, far_other)
    )
    far_weight_3 = send(weight_3, WRAP)
    far_weight_4 = send(weight_4, PARTNER)
    other = send(mine, OTHER_CORE)

    hidden = [hidden_rows, far_hidden_0, far_hidden_1, far_hidden_2]
    keep, away, gram = right_part(core_arg, mine, other, err, hidden, masked_own, masked_other)
    total = keep + send(away, OTHER_CORE)
    total, gram = barrier((total, gram))
    factor_low = jnp.linalg.cholesky(gram)
    total = sum_of_four(total, "y")
    total, factor_low, far_weight_3, far_weight_4 = barrier((total, factor_low, far_weight_3, far_weight_4))
    pieces = [far_weight_0, far_weight_1, far_weight_2, far_weight_3, far_weight_4]
    grad, grad_other = input_part(core_arg, masked_own, near_other, masked_far, far_other, key_weight, pieces)
    total = sum_of_four(total, "z")
    total, factor_low, grad_other = barrier((total, factor_low, grad_other))
    inverse = jax.scipy.linalg.solve_triangular(factor_low, jnp.eye(64, dtype=F32), lower=True)
    grad_far = send(grad_other, OTHER_CORE)
    total = total + send(total, permutation(x=2))
    total_other = send(total, OTHER_CORE)

    update, new_error, factor, input_grad = final_part(
        core_arg, masked_own, masked_other, total, total_other, inverse, grad_far, grad, mine, other, err, hidden
    )
    return input_grad, update, new_error[None], factor.T


def solution(mesh):
    fine = Mesh(mesh.devices.reshape(SIZES), AXES)
    dp = ("z", "y", "xh", "core")
    placed = (
        P(AXES, None),
        P(dp, "xl"),
        P(dp),
        P(None, "xl"),
        P(dp, None, "xl"),
        P("xl", None),
    )
    return jax.shard_map(
        local,
        mesh=fine,
        in_specs=placed,
        out_specs=(P(AXES, None), P(None, "xl"), P(dp, None, "xl"), P("xl", None)),
        check_vma=False,
    )
```

```python
import functools

import jax
import jax.numpy as jnp
import numpy as np
from jax import lax
from jax.experimental import pallas as pl
from jax.experimental.pallas import tpu as pltpu
from jax.sharding import Mesh
from jax.sharding import PartitionSpec as P

AXES = ("z", "y", "xh", "core", "xl")
SIZES = (4, 4, 2, 2, 2)
BF = jnp.bfloat16
F32 = jnp.float32
HIGHEST = lax.Precision.HIGHEST
BLK = 512
AHEAD = 4
SLOTS = 16
COUNT = 8192 // BLK
HALF = COUNT // 2


def permutation(z=0, y=0, x=0, core=0, pairs=None):
    result = []
    for source in range(128):
        cz, cy, ch, cc, cl = (int(v) for v in np.unravel_index(source, SIZES))
        place = {"z": cz, "y": cy, "x": ch * 2 + cl}
        if pairs is not None:
            place[pairs[0]] = ((1, 0, 3, 2), (3, 2, 1, 0))[pairs[1]][place[pairs[0]]]
        cz, cy, cx = (place["z"] + z) % 4, (place["y"] + y) % 4, (place["x"] + x) % 4
        target = (cz, cy, cx // 2, (cc + core) % 2, cx % 2)
        result.append((source, int(np.ravel_multi_index(target, SIZES))))
    return result


OTHER_CORE = permutation(core=1)
PARTNER = permutation(pairs=("x", 0))
WRAP = permutation(pairs=("x", 1))


def send(array, pairs):
    return lax.ppermute(array, AXES, pairs)


def sum_of_four(array, axis):
    ahead = send(array, permutation(**{axis: 1}))
    behind = send(array, permutation(**{axis: 3}))
    across = send(array, permutation(**{axis: 2}))
    return (array + across) + (ahead + behind)


def kernel_split3(value):
    a = value.astype(BF)
    rest = value - a.astype(F32)
    b = rest.astype(BF)
    c = (rest - b.astype(F32)).astype(BF)
    return a, b, c


def stack3(value):
    return jnp.concatenate(kernel_split3(value), axis=0)


def sum3(value):
    return value[:64] + value[64:128] + value[128:192]


def dot(a, b, contract):
    return lax.dot_general(a, b, ((contract[:1], contract[1:]), ((), ())), preferred_element_type=F32)


def start(copies):
    for copy in copies:
        copy.start()


def wait(copies):
    for copy in copies:
        copy.wait()


def call(kernel, name, operands, outs, scratch, limit, aliases=None, hbm=False, loose=()):
    anywhere = pl.BlockSpec(memory_space=pl.ANY)
    far = [
        array if number in loose else pltpu.with_memory_space_constraint(array, pltpu.HBM)
        for number, array in enumerate(operands[1:], 1)
    ]
    return pl.pallas_call(
        kernel,
        out_shape=[(pltpu.HBM if hbm else jax.ShapeDtypeStruct)(shape, dtype) for shape, dtype in outs],
        in_specs=[pl.BlockSpec(memory_space=pltpu.SMEM)] + [anywhere if n in loose else pl.BlockSpec(memory_space=pltpu.HBM) for n in range(1, len(operands))],
        out_specs=[anywhere] * len(outs),
        scratch_shapes=scratch,
        input_output_aliases=aliases or {},
        compiler_params=pltpu.CompilerParams(vmem_limit_bytes=limit * 2**20),
        cost_estimate=pl.CostEstimate(flops=1024, bytes_accessed=1024, transcendentals=0),
        name=name,
    )(operands[0], *far)


def rows_of(block):
    return pl.ds(pl.multiple_of(block * BLK, BLK), BLK)


def error_loads(err, v_err, sems, places):
    return [pltpu.make_async_copy(err.at[rows_of(p), :], v_err.at[p], sems.at[j]) for j, p in enumerate(places)]


class Group:
    def __init__(self, copies):
        self.copies = copies

    def start(self):
        start(self.copies)

    def wait(self):
        wait(self.copies)


def hidden_loads(hidden, v_hid, sems, places):
    groups = []
    for j, place in enumerate(places):
        copies, row = [], 0
        for number, part in enumerate(hidden):
            size = part.shape[0]
            copies.append(
                pltpu.make_async_copy(part.at[:, rows_of(place)], v_hid.at[place, pl.ds(row, size), :], sems.at[j, number])
            )
            row += size
        groups.append(Group(copies))
    return groups


def factor_loads(mine, other, v_left, sems, places):
    return [
        pltpu.make_async_copy((mine, other)[j // HALF].at[pl.ds(2 * (j % HALF), 2)], v_left.at[p], sems.at[j])
        for j, p in enumerate(places)
    ]


def token_kernel(
    xl_ref, grads, mask, factor_t, own, other, tok_own, tok_other, terms_t, v_grads, v_mask, v_factor, v_tok, v_masked, v_terms, sems
):
    loads = [
        pltpu.make_async_copy(grads, v_grads, sems.at[0]),
        pltpu.make_async_copy(mask, v_mask, sems.at[1]),
        pltpu.make_async_copy(factor_t, v_factor, sems.at[2]),
    ]
    start(loads)
    wait(loads)
    flags = jnp.broadcast_to(v_mask[...].astype(F32), (128, 256)).T[:, :1]
    masked = (v_grads[...].astype(F32) * flags).astype(BF)
    terms = stack3(v_factor[...])
    tok = sum3(dot(terms, masked, (1, 1))) * (1.0 / 16.0)
    first = xl_ref[0] == 0
    v_tok[0] = jnp.where(first, tok[:, 128:], tok[:, :128])
    v_tok[1] = jnp.where(first, tok[:, :128], tok[:, 128:])
    v_terms[...] = terms
    v_masked[0] = jnp.where(first, masked[:128], masked[128:])
    v_masked[1] = jnp.where(first, masked[128:], masked[:128])
    stores = [
        pltpu.make_async_copy(v_tok.at[0], tok_other, sems.at[3]),
        pltpu.make_async_copy(v_tok.at[1], tok_own, sems.at[4]),
        pltpu.make_async_copy(v_terms, terms_t, sems.at[5]),
        pltpu.make_async_copy(v_masked.at[0], own, sems.at[6]),
        pltpu.make_async_copy(v_masked.at[1], other, sems.at[7]),
    ]
    start(stores)
    wait(stores)


def token_part(xl, grads, mask, factor_t):
    return call(
        token_kernel,
        "token_part",
        (xl, grads, mask, factor_t),
        [((128, 512), BF), ((128, 512), BF), ((64, 128), F32), ((64, 128), F32), ((192, 512), BF)],
        [
            pltpu.VMEM((256, 512), BF),
            pltpu.VMEM((1, 256), jnp.int32),
            pltpu.VMEM((64, 512), F32),
            pltpu.VMEM((2, 64, 128), F32),
            pltpu.VMEM((2, 128, 512), BF),
            pltpu.VMEM((192, 512), BF),
            pltpu.SemaphoreType.DMA((8,)),
        ],
        8,
        hbm=True,
    )


def parcel_kernel(firsts, core_ref, after, hidden, key_weight, *refs):
    count = len(firsts)
    parcels, v_parcels, sems = refs[:count], refs[count : 2 * count], refs[2 * count]
    picks, drops = [], []
    for k, (kind, first) in enumerate(firsts):
        rows = parcels[k].shape[0]
        if kind == "hidden":
            source = hidden.at[pl.ds(first, rows), :]
        else:
            source = key_weight.at[pl.ds(pl.multiple_of(core_ref[0] * 4096 + first, 64), rows), :]
        picks.append(pltpu.make_async_copy(source, v_parcels[k], sems.at[0, k]))
        drops.append(pltpu.make_async_copy(v_parcels[k], parcels[k], sems.at[1, k]))
    start(picks)
    for pick, drop in zip(picks, drops):
        pick.wait()
        drop.start()
    wait(drops)


def parcel_part(core, after, hidden, key_weight, parcels):
    shapes = [((rows, 8192 if kind == "hidden" else 512), BF) for kind, _, rows in parcels]
    return call(
        functools.partial(parcel_kernel, [(kind, first) for kind, first, _ in parcels]),
        "parcel_part",
        (core, after, hidden, key_weight),
        shapes,
        [*[pltpu.VMEM(shape, dtype) for shape, dtype in shapes], pltpu.SemaphoreType.DMA((2, len(shapes)))],
        10,
        hbm=True,
    )


def left_kernel(
    core_ref, err, hidden, terms_t, tok_own, tok_far, keep, away, v_err, v_hid, v_terms, v_tok, v_out, sems, sem_err, sem_hid, sem_out
):
    small = [
        pltpu.make_async_copy(terms_t, v_terms, sems.at[0]),
        pltpu.make_async_copy(tok_own, v_tok.at[0], sems.at[1]),
        pltpu.make_async_copy(tok_far, v_tok.at[1], sems.at[2]),
    ]
    places = [(1 - core_ref[0]) * HALF + j if j < HALF else core_ref[0] * HALF + j - HALF for j in range(COUNT)]
    loads = list(zip(error_loads(err, v_err, sem_err, places), hidden_loads([hidden], v_hid, sem_hid, places)))
    start(small)
    for j in range(AHEAD):
        start(loads[j])
    wait(small)
    toks = stack3(v_tok[0] + v_tok[1])
    stores = []
    for j in range(COUNT):
        wait(loads[j])
        if j + AHEAD < COUNT:
            start(loads[j + AHEAD])
        value = sum3(dot(v_terms[...], v_err[places[j]], (1, 1)) + dot(toks, v_hid[places[j]], (1, 0)))
        v_out[j, 0] = value[:, :256]
        v_out[j, 1] = value[:, 256:]
        target = away if j < HALF else keep
        stores.append(pltpu.make_async_copy(v_out.at[j], target.at[pl.ds(2 * (j % HALF), 2)], sem_out.at[j]))
        stores[j].start()
    wait(stores)


def left_part(core, err, hidden, terms_t, tok_own, tok_far):
    return call(
        left_kernel,
        "left_part",
        (core, err, hidden, terms_t, tok_own, tok_far),
        [((16, 64, 256), F32), ((16, 64, 256), F32)],
        [
            pltpu.VMEM((COUNT, BLK, 512), BF),
            pltpu.VMEM((COUNT, 128, BLK), BF),
            pltpu.VMEM((192, 512), BF),
            pltpu.VMEM((2, 64, 128), F32),
            pltpu.VMEM((COUNT, 2, 64, 256), F32),
            pltpu.SemaphoreType.DMA((3,)),
            pltpu.SemaphoreType.DMA((COUNT,)),
            pltpu.SemaphoreType.DMA((COUNT, 1)),
            pltpu.SemaphoreType.DMA((COUNT,)),
        ],
        28,
    )


def right_kernel(count, core_ref, mine, other, err, masked_own, masked_other, *refs):
    hidden = refs[:count]
    keep, away, gram, v_left, v_err, v_hid = refs[count : count + 6]
    v_masked, v_keep, v_away, v_gram, sems, sem_left, sem_err, sem_hid = refs[count + 6 :]
    places = [core_ref[0] * HALF + j if j < HALF else (1 - core_ref[0]) * HALF + j - HALF for j in range(COUNT)]
    loads = list(
        zip(
            factor_loads(mine, other, v_left, sem_left, places),
            error_loads(err, v_err, sem_err, places),
            hidden_loads(hidden, v_hid, sem_hid, places),
        )
    )
    late = [
        pltpu.make_async_copy(masked_own, v_masked.at[pl.ds(0, 128), :], sems.at[0]),
        pltpu.make_async_copy(masked_other, v_masked.at[pl.ds(128, 128), :], sems.at[4]),
    ]
    for j in range(AHEAD):
        start(loads[j])
    start(late)
    w_sum, g_sum, z_sum = 0.0, 0.0, 0.0
    for j in range(COUNT):
        wait(loads[j])
        if j + AHEAD < COUNT:
            start(loads[j + AHEAD])
        terms = stack3(jnp.concatenate([v_left[places[j], 0], v_left[places[j], 1]], axis=1))
        w_sum = w_sum + dot(terms, v_err[places[j]], (1, 0))
        g_sum = g_sum + dot(terms, terms, (1, 1))
        z_sum = z_sum + dot(terms, v_hid[places[j]], (1, 1))
    wait(late)
    z = sum3(z_sum) * (1.0 / 16.0)
    right = sum3(w_sum + dot(stack3(z), v_masked[...], (1, 0)))
    first = core_ref[0] == 0
    v_keep[...] = jnp.where(first, right[:32], right[32:])
    v_away[...] = jnp.where(first, right[32:], right[:32])
    g = sum3(g_sum)
    v_gram[...] = g[:, :64] + g[:, 64:128] + g[:, 128:192]
    stores = [
        pltpu.make_async_copy(v_away, away, sems.at[1]),
        pltpu.make_async_copy(v_keep, keep, sems.at[2]),
        pltpu.make_async_copy(v_gram, gram, sems.at[3]),
    ]
    start(stores)
    wait(stores)


def right_part(core, mine, other, err, hidden, masked_own, masked_other):
    return call(
        functools.partial(right_kernel, len(hidden)),
        "right_part",
        (core, mine, other, err, masked_own, masked_other, *hidden),
        [((32, 512), F32), ((32, 512), F32), ((64, 64), F32)],
        [
            pltpu.VMEM((COUNT, 2, 64, 256), F32),
            pltpu.VMEM((COUNT, BLK, 512), BF),
            pltpu.VMEM((COUNT, 256, BLK), BF),
            pltpu.VMEM((256, 512), BF),
            pltpu.VMEM((32, 512), F32),
            pltpu.VMEM((32, 512), F32),
            pltpu.VMEM((64, 64), F32),
            pltpu.SemaphoreType.DMA((5,)),
            pltpu.SemaphoreType.DMA((COUNT,)),
            pltpu.SemaphoreType.DMA((COUNT,)),
            pltpu.SemaphoreType.DMA((COUNT, len(hidden))),
        ],
        28,
    )


def inverse_kernel(gram, inverse):
    both = jnp.concatenate([gram[...], jnp.eye(64, dtype=F32)], axis=1)
    rows = lax.broadcasted_iota(jnp.int32, (64, 1), 0)
    scale = jnp.zeros((64, 1), F32)
    for j in range(64):
        pivot = both[j : j + 1, j : j + 1]
        scale = jnp.where(rows == j, pivot, scale)
        factor = jnp.where(rows > j, both[:, j : j + 1], 0.0) / pivot
        both = both - factor * both[j : j + 1, :]
    inverse[...] = both[:, 64:] / jnp.sqrt(scale)


def inverse_part(gram):
    return pl.pallas_call(
        inverse_kernel,
        out_shape=jax.ShapeDtypeStruct((64, 64), F32),
        cost_estimate=pl.CostEstimate(flops=1024, bytes_accessed=1024, transcendentals=0),
        name="inverse_part",
    )(gram)


def final_kernel(
    count, core_ref, masked_own, masked_other, total, total_other, inverse, grad_far, grad_base, mine, other, err, *refs
):
    hidden, refs = refs[:count], refs[count:]
    update, new_error, factor, grad = refs[:4]
    v_left, v_err, v_hid, v_masked, v_right, v_inv, v_factor, v_update, v_new, v_grad = refs[4:14]
    sems, sem_left, sem_err, sem_hid, sem_out = refs[14:]
    core = core_ref[0]
    places = [core * HALF + j if j < HALF else (1 - core) * HALF + j - HALF for j in range(COUNT)]
    loads = list(
        zip(
            factor_loads(mine, other, v_left, sem_left, places),
            error_loads(err, v_err, sem_err, places),
            hidden_loads(hidden, v_hid, sem_hid, places),
        )
    )
    small = [
        pltpu.make_async_copy(inverse, v_inv, sems.at[0]),
        pltpu.make_async_copy(total, v_right.at[pl.ds(pl.multiple_of(core * 32, 32), 32), :], sems.at[1]),
        pltpu.make_async_copy(total_other, v_right.at[pl.ds(pl.multiple_of((1 - core) * 32, 32), 32), :], sems.at[2]),
        pltpu.make_async_copy(masked_own, v_masked.at[pl.ds(0, 128), :], sems.at[3]),
        pltpu.make_async_copy(masked_other, v_masked.at[pl.ds(128, 128), :], sems.at[7]),
    ]
    grad_in = pltpu.make_async_copy(grad_far, v_grad, sems.at[4])
    start(small)
    for j in range(AHEAD):
        start(loads[j])
    wait(small)
    v_factor[...] = jnp.dot(v_inv[...], v_right[...], precision=HIGHEST, preferred_element_type=F32) * (1.0 / 64.0)
    coefficients = lax.dot_general(
        v_inv[...], v_factor[...], (((0,), (0,)), ((), ())), precision=HIGHEST, preferred_element_type=F32
    )
    y1, y2, y3 = kernel_split3(coefficients)
    ys = jnp.concatenate([y1, y1, y1, y2, y2, y3], axis=0)
    stores = [pltpu.make_async_copy(v_factor, factor, sems.at[5])]
    stores[0].start()
    for j in range(COUNT):
        place = places[j]
        wait(loads[j])
        if j + AHEAD < COUNT:
            start(loads[j + AHEAD])
        elif j + AHEAD == COUNT:
            grad_in.start()
        l1, l2, l3 = kernel_split3(jnp.concatenate([v_left[place, 0], v_left[place, 1]], axis=1))
        estimate = dot(jnp.concatenate([l1, l2, l3, l1, l2, l1], axis=0), ys, (0, 0))
        merged = dot(v_hid[place], v_masked[...], (0, 0)) * (1.0 / 16.0) + v_err[place].astype(F32)
        slot = j % SLOTS
        if j >= SLOTS:
            wait(stores[2 * (j - SLOTS) + 1 : 2 * (j - SLOTS) + 3])
        v_update[slot] = estimate.astype(BF)
        v_new[slot] = (merged - estimate).astype(BF)
        for k, (source, target) in enumerate(((v_update, update), (v_new, new_error))):
            copy = pltpu.make_async_copy(source.at[slot], target.at[rows_of(place), :], sem_out.at[k, slot])
            copy.start()
            stores.append(copy)
    grad_in.wait()
    columns = pl.ds(pl.multiple_of((1 - core) * 4096, 4096), 4096)
    stores.append(pltpu.make_async_copy(v_grad, grad.at[:, columns], sems.at[6]))
    stores[-1].start()
    wait(stores[:1] + stores[2 * (COUNT - SLOTS) + 1 :])


def final_part(core, masked_own, masked_other, total, total_other, inverse, grad_far, grad_base, mine, other, err, hidden):
    return call(
        functools.partial(final_kernel, len(hidden)),
        "final_part",
        (core, masked_own, masked_other, total, total_other, inverse, grad_far, grad_base, mine, other, err, *hidden),
        [((8192, 512), BF), ((8192, 512), BF), ((64, 512), F32), ((128, 8192), BF)],
        [
            pltpu.VMEM((COUNT, 2, 64, 256), F32),
            pltpu.VMEM((COUNT, BLK, 512), BF),
            pltpu.VMEM((COUNT, 256, BLK), BF),
            pltpu.VMEM((256, 512), BF),
            pltpu.VMEM((64, 512), F32),
            pltpu.VMEM((64, 64), F32),
            pltpu.VMEM((64, 512), F32),
            pltpu.VMEM((SLOTS, BLK, 512), BF),
            pltpu.VMEM((SLOTS, BLK, 512), BF),
            pltpu.VMEM((128, 4096), BF),
            pltpu.SemaphoreType.DMA((8,)),
            pltpu.SemaphoreType.DMA((COUNT,)),
            pltpu.SemaphoreType.DMA((COUNT,)),
            pltpu.SemaphoreType.DMA((COUNT, len(hidden))),
            pltpu.SemaphoreType.DMA((2, SLOTS)),
        ],
        44,
        aliases={7: 3},
        loose=(3, 4, 5, 6),
    )


def input_kernel(count, core_ref, near_own, near_other, far_own, far_other, key_weight, *refs):
    pieces = refs[:count]
    grad, grad_other, v_near, v_far, v_wnear, v_wfar, v_own, v_other, sems, sem_near, sem_far, sem_out = refs[count:]
    core = core_ref[0]
    small = [
        pltpu.make_async_copy(near_own, v_near.at[pl.ds(0, 128), :], sems.at[0]),
        pltpu.make_async_copy(near_other, v_near.at[pl.ds(128, 128), :], sems.at[1]),
        pltpu.make_async_copy(far_own, v_far.at[pl.ds(0, 128), :], sems.at[2]),
        pltpu.make_async_copy(far_other, v_far.at[pl.ds(128, 128), :], sems.at[3]),
    ]
    loads, fars, ends, row = [], [], [], 0
    for j in range(4):
        place = pl.ds(pl.multiple_of(core * 4096 + j * 1024, 1024), 1024)
        loads.append(pltpu.make_async_copy(key_weight.at[place, :], v_wnear.at[j], sem_near.at[j]))
    for number, piece in enumerate(pieces):
        size = piece.shape[0]
        fars.append(pltpu.make_async_copy(piece, v_wfar.at[pl.ds(row, size), :], sem_far.at[number]))
        row += size
        ends.append(row)
    start(small)
    begun = 0
    for j in range(4):
        loads[j].start()
        while begun < count and (0 if begun == 0 else ends[begun - 1]) < (j + 1) * 1024:
            fars[begun].start()
            begun += 1
    wait(small)
    stores, waited = [], 0
    for j in range(4):
        loads[j].wait()
        while waited < count and (0 if waited == 0 else ends[waited - 1]) < (j + 1) * 1024:
            fars[waited].wait()
            waited += 1
        value = dot(v_near[...], v_wnear[j], (1, 1))
        value = (value + dot(v_far[...], v_wfar[pl.ds(j * 1024, 1024), :], (1, 1))).astype(BF)
        v_own[j] = value[:128]
        v_other[j] = value[128:]
        place = pl.ds(pl.multiple_of(core * 4096 + j * 1024, 1024), 1024)
        stores.append(pltpu.make_async_copy(v_own.at[j], grad.at[:, place], sem_out.at[0, j]))
        stores.append(pltpu.make_async_copy(v_other.at[j], grad_other.at[:, pl.ds(j * 1024, 1024)], sem_out.at[1, j]))
        start(stores[-2:])
    wait(stores)


def input_part(core, near_own, near_other, far_own, far_other, key_weight, pieces):
    return call(
        functools.partial(input_kernel, len(pieces)),
        "input_part",
        (core, near_own, near_other, far_own, far_other, key_weight, *pieces),
        [((128, 8192), BF), ((128, 4096), BF)],
        [
            pltpu.VMEM((256, 512), BF),
            pltpu.VMEM((256, 512), BF),
            pltpu.VMEM((4, 1024, 512), BF),
            pltpu.VMEM((4096, 512), BF),
            pltpu.VMEM((4, 128, 1024), BF),
            pltpu.VMEM((4, 128, 1024), BF),
            pltpu.SemaphoreType.DMA((4,)),
            pltpu.SemaphoreType.DMA((4,)),
            pltpu.SemaphoreType.DMA((len(pieces),)),
            pltpu.SemaphoreType.DMA((2, 4)),
        ],
        18,
    )


def local(hidden_rows, key_grads, loss_mask, key_weight, error_buf, right_factor):
    core = lax.axis_index("core")
    core_arg = core.astype(jnp.int32)[None]
    xl_arg = lax.axis_index("xl").astype(jnp.int32)[None]
    err = error_buf.reshape(8192, 512)
    barrier = lax.optimization_barrier

    def weight_rows(first, rows):
        return lax.dynamic_slice(key_weight, (core * 4096 + first, 0), (rows, 512))

    masked_own, masked_other, tok_own, tok_other, terms_t = token_part(
        xl_arg, key_grads, loss_mask.reshape(1, 256), right_factor.T
    )

    tok_far = send(tok_other, PARTNER)

    lots = [("hidden", 0, 16), ("hidden", 16, 80), ("hidden", 96, 32)]
    first = 0
    for rows in (448, 1152, 448, 1024, 1024):
        lots.append(("weight", first, rows))
        first += rows
    parcels = parcel_part(core_arg, masked_own, hidden_rows, key_weight, lots)
    parcels, weights = list(parcels[:3]), list(parcels[3:])
    tok_far, parcels[0], weights[0], masked_other = barrier((tok_far, parcels[0], weights[0], masked_other))
    masked_far = send(masked_other, PARTNER)
    far_hidden = [send(parcels[0], PARTNER)]
    far_weight = [send(weights[0], WRAP)]

    keep, away = left_part(core_arg, err, hidden_rows, terms_t, tok_own, tok_far)
    keep, away, far_hidden[0], far_weight[0], parcels[1], weights[1], masked_far = barrier(
        (keep, away, far_hidden[0], far_weight[0], parcels[1], weights[1], masked_far)
    )
    piece = keep + send(away, OTHER_CORE)
    far_hidden.append(send(parcels[1], PARTNER))
    far_weight.append(send(weights[1], WRAP))
    far_hidden[1], far_weight[1], masked_own = barrier((far_hidden[1], far_weight[1], masked_own))
    near_other = send(masked_own, OTHER_CORE)
    piece = lax.all_to_all(piece, ("z", "y"), 0, 0, tiled=True)
    piece = jnp.sum(piece, axis=0)
    piece, near_other = barrier((piece, near_other))
    piece = sum_of_four(piece, "x")

    piece, parcels[2], weights[2], masked_far = barrier((piece, parcels[2], weights[2], masked_far))
    far_hidden.append(send(parcels[2], PARTNER))
    far_weight.append(send(weights[2], WRAP))
    far_other = send(masked_far, OTHER_CORE)
    mine = lax.all_to_all(jnp.broadcast_to(piece[None], (16, 64, 256)), ("z", "y"), 0, 0, tiled=True)
    mine, far_hidden[2], far_weight[2], weights[3], weights[4], far_other = barrier(
        (mine, far_hidden[2], far_weight[2], weights[3], weights[4], far_other)
    )
    far_weight.append(send(weights[3], WRAP))
    far_weight.append(send(weights[4], PARTNER))
    other = send(mine, OTHER_CORE)

    hidden = [hidden_rows, *far_hidden]
    keep, away, gram = right_part(core_arg, mine, other, err, hidden, masked_own, masked_other)
    total = keep + send(away, OTHER_CORE)
    total, gram = barrier((total, gram))
    inverse = inverse_part(gram)
    total = sum_of_four(total, "y")
    total, inverse, far_weight[3], far_weight[4] = barrier((total, inverse, far_weight[3], far_weight[4]))
    grad, grad_other = input_part(core_arg, masked_own, near_other, masked_far, far_other, key_weight, far_weight)
    total = sum_of_four(total, "z")
    total, grad_other = barrier((total, grad_other))
    grad_far = send(grad_other, OTHER_CORE)
    total = total + send(total, permutation(x=2))
    total_other = send(total, OTHER_CORE)

    update, new_error, factor, input_grad = final_part(
        core_arg, masked_own, masked_other, total, total_other, inverse, grad_far, grad, mine, other, err, hidden
    )
    return input_grad, update, new_error[None], factor.T


def solution(mesh):
    fine = Mesh(mesh.devices.reshape(SIZES), AXES)
    dp = ("z", "y", "xh", "core")
    placed = (
        P(AXES, None),
        P(dp, "xl"),
        P(dp),
        P(None, "xl"),
        P(dp, None, "xl"),
        P("xl", None),
    )
    return jax.shard_map(
        local,
        mesh=fine,
        in_specs=placed,
        out_specs=(P(AXES, None), P(None, "xl"), P(dp, None, "xl"), P("xl", None)),
        check_vma=False,
    )
```

```python
import functools

import jax
import jax.numpy as jnp
import numpy as np
from jax import lax
from jax.experimental import pallas as pl
from jax.experimental.pallas import tpu as pltpu
from jax.sharding import Mesh
from jax.sharding import PartitionSpec as P

AXES = ("z", "y", "xh", "core", "xl")
SIZES = (4, 4, 2, 2, 2)
BF = jnp.bfloat16
F32 = jnp.float32
HIGHEST = lax.Precision.HIGHEST
BLK = 512
AHEAD = 4
SLOTS = 16
COUNT = 8192 // BLK
HALF = COUNT // 2


def permutation(z=0, y=0, x=0, core=0, pairs=None):
    result = []
    for source in range(128):
        cz, cy, ch, cc, cl = (int(v) for v in np.unravel_index(source, SIZES))
        place = {"z": cz, "y": cy, "x": ch * 2 + cl}
        if pairs is not None:
            place[pairs[0]] = ((1, 0, 3, 2), (3, 2, 1, 0))[pairs[1]][place[pairs[0]]]
        cz, cy, cx = (place["z"] + z) % 4, (place["y"] + y) % 4, (place["x"] + x) % 4
        target = (cz, cy, cx // 2, (cc + core) % 2, cx % 2)
        result.append((source, int(np.ravel_multi_index(target, SIZES))))
    return result


OTHER_CORE = permutation(core=1)
PARTNER = permutation(pairs=("x", 0))
WRAP = permutation(pairs=("x", 1))


def send(array, pairs):
    return lax.ppermute(array, AXES, pairs)


def sum_of_four(array, axis):
    ahead = send(array, permutation(**{axis: 1}))
    behind = send(array, permutation(**{axis: 3}))
    across = send(array, permutation(**{axis: 2}))
    return (array + across) + (ahead + behind)


def kernel_split3(value):
    a = value.astype(BF)
    rest = value - a.astype(F32)
    b = rest.astype(BF)
    c = (rest - b.astype(F32)).astype(BF)
    return a, b, c


def stack3(value):
    return jnp.concatenate(kernel_split3(value), axis=0)


def sum3(value):
    return value[:64] + value[64:128] + value[128:192]


def dot(a, b, contract):
    return lax.dot_general(a, b, ((contract[:1], contract[1:]), ((), ())), preferred_element_type=F32)


def start(copies):
    for copy in copies:
        copy.start()


def wait(copies):
    for copy in copies:
        copy.wait()


def call(kernel, name, operands, outs, scratch, limit, aliases=None, hbm=False, loose=()):
    anywhere = pl.BlockSpec(memory_space=pl.ANY)
    far = [
        array if number in loose else pltpu.with_memory_space_constraint(array, pltpu.HBM)
        for number, array in enumerate(operands[1:], 1)
    ]
    return pl.pallas_call(
        kernel,
        out_shape=[(pltpu.HBM if hbm else jax.ShapeDtypeStruct)(shape, dtype) for shape, dtype in outs],
        in_specs=[pl.BlockSpec(memory_space=pltpu.SMEM)] + [anywhere if n in loose else pl.BlockSpec(memory_space=pltpu.HBM) for n in range(1, len(operands))],
        out_specs=[anywhere] * len(outs),
        scratch_shapes=scratch,
        input_output_aliases=aliases or {},
        compiler_params=pltpu.CompilerParams(vmem_limit_bytes=limit * 2**20),
        cost_estimate=pl.CostEstimate(flops=1024, bytes_accessed=1024, transcendentals=0),
        name=name,
    )(operands[0], *far)


def rows_of(block):
    return pl.ds(pl.multiple_of(block * BLK, BLK), BLK)


def error_loads(err, v_err, sems, places):
    return [pltpu.make_async_copy(err.at[rows_of(p), :], v_err.at[p], sems.at[j]) for j, p in enumerate(places)]


class Group:
    def __init__(self, copies):
        self.copies = copies

    def start(self):
        start(self.copies)

    def wait(self):
        wait(self.copies)


def hidden_loads(hidden, v_hid, sems, places):
    groups = []
    for j, place in enumerate(places):
        copies, row = [], 0
        for number, part in enumerate(hidden):
            size = part.shape[0]
            copies.append(
                pltpu.make_async_copy(part.at[:, rows_of(place)], v_hid.at[place, pl.ds(row, size), :], sems.at[j, number])
            )
            row += size
        groups.append(Group(copies))
    return groups


def factor_loads(mine, other, v_left, sems, places):
    return [
        pltpu.make_async_copy((mine, other)[j // HALF].at[pl.ds(2 * (j % HALF), 2)], v_left.at[p], sems.at[j])
        for j, p in enumerate(places)
    ]


def token_kernel(
    xl_ref, grads, mask, factor_t, own, other, tok_own, tok_other, terms_t, v_grads, v_mask, v_factor, v_tok, v_masked, v_terms, sems
):
    loads = [
        pltpu.make_async_copy(grads, v_grads, sems.at[0]),
        pltpu.make_async_copy(mask, v_mask, sems.at[1]),
        pltpu.make_async_copy(factor_t, v_factor, sems.at[2]),
    ]
    start(loads)
    wait(loads)
    flags = jnp.broadcast_to(v_mask[...].astype(F32), (128, 256)).T[:, :1]
    masked = (v_grads[...].astype(F32) * flags).astype(BF)
    terms = stack3(v_factor[...])
    tok = sum3(dot(terms, masked, (1, 1))) * (1.0 / 16.0)
    first = xl_ref[0] == 0
    v_tok[0] = jnp.where(first, tok[:, 128:], tok[:, :128])
    v_tok[1] = jnp.where(first, tok[:, :128], tok[:, 128:])
    v_terms[...] = terms
    v_masked[0] = jnp.where(first, masked[:128], masked[128:])
    v_masked[1] = jnp.where(first, masked[128:], masked[:128])
    stores = [
        pltpu.make_async_copy(v_tok.at[0], tok_other, sems.at[3]),
        pltpu.make_async_copy(v_tok.at[1], tok_own, sems.at[4]),
        pltpu.make_async_copy(v_terms, terms_t, sems.at[5]),
        pltpu.make_async_copy(v_masked.at[0], own, sems.at[6]),
        pltpu.make_async_copy(v_masked.at[1], other, sems.at[7]),
    ]
    start(stores)
    wait(stores)


def token_part(xl, grads, mask, factor_t):
    return call(
        token_kernel,
        "token_part",
        (xl, grads, mask, factor_t),
        [((128, 512), BF), ((128, 512), BF), ((64, 128), F32), ((64, 128), F32), ((192, 512), BF)],
        [
            pltpu.VMEM((256, 512), BF),
            pltpu.VMEM((1, 256), jnp.int32),
            pltpu.VMEM((64, 512), F32),
            pltpu.VMEM((2, 64, 128), F32),
            pltpu.VMEM((2, 128, 512), BF),
            pltpu.VMEM((192, 512), BF),
            pltpu.SemaphoreType.DMA((8,)),
        ],
        8,
        hbm=True,
    )


def parcel_kernel(firsts, core_ref, after, hidden, key_weight, *refs):
    count = len(firsts)
    parcels, v_parcels, sems = refs[:count], refs[count : 2 * count], refs[2 * count]
    picks, drops = [], []
    for k, (kind, first) in enumerate(firsts):
        rows = parcels[k].shape[0]
        if kind == "hidden":
            source = hidden.at[pl.ds(first, rows), :]
        else:
            source = key_weight.at[pl.ds(pl.multiple_of(core_ref[0] * 4096 + first, 64), rows), :]
        picks.append(pltpu.make_async_copy(source, v_parcels[k], sems.at[0, k]))
        drops.append(pltpu.make_async_copy(v_parcels[k], parcels[k], sems.at[1, k]))
    start(picks)
    for pick, drop in zip(picks, drops):
        pick.wait()
        drop.start()
    wait(drops)


def parcel_part(core, after, hidden, key_weight, parcels):
    shapes = [((rows, 8192 if kind == "hidden" else 512), BF) for kind, _, rows in parcels]
    return call(
        functools.partial(parcel_kernel, [(kind, first) for kind, first, _ in parcels]),
        "parcel_part",
        (core, after, hidden, key_weight),
        shapes,
        [*[pltpu.VMEM(shape, dtype) for shape, dtype in shapes], pltpu.SemaphoreType.DMA((2, len(shapes)))],
        10,
        hbm=True,
    )


def left_kernel(
    core_ref, err, hidden, terms_t, tok_own, tok_far, keep, away, v_err, v_hid, v_terms, v_tok, v_out, sems, sem_err, sem_hid, sem_out
):
    small = [
        pltpu.make_async_copy(terms_t, v_terms, sems.at[0]),
        pltpu.make_async_copy(tok_own, v_tok.at[0], sems.at[1]),
        pltpu.make_async_copy(tok_far, v_tok.at[1], sems.at[2]),
    ]
    places = [(1 - core_ref[0]) * HALF + j if j < HALF else core_ref[0] * HALF + j - HALF for j in range(COUNT)]
    loads = list(zip(error_loads(err, v_err, sem_err, places), hidden_loads([hidden], v_hid, sem_hid, places)))
    start(small)
    for j in range(AHEAD):
        start(loads[j])
    wait(small)
    toks = stack3(v_tok[0] + v_tok[1])
    stores = []
    for j in range(COUNT):
        wait(loads[j])
        if j + AHEAD < COUNT:
            start(loads[j + AHEAD])
        value = sum3(dot(v_terms[...], v_err[places[j]], (1, 1)) + dot(toks, v_hid[places[j]], (1, 0)))
        v_out[j, 0] = value[:, :256]
        v_out[j, 1] = value[:, 256:]
        target = away if j < HALF else keep
        stores.append(pltpu.make_async_copy(v_out.at[j], target.at[pl.ds(2 * (j % HALF), 2)], sem_out.at[j]))
        stores[j].start()
    wait(stores)


def left_part(core, err, hidden, terms_t, tok_own, tok_far):
    return call(
        left_kernel,
        "left_part",
        (core, err, hidden, terms_t, tok_own, tok_far),
        [((16, 64, 256), F32), ((16, 64, 256), F32)],
        [
            pltpu.VMEM((COUNT, BLK, 512), BF),
            pltpu.VMEM((COUNT, 128, BLK), BF),
            pltpu.VMEM((192, 512), BF),
            pltpu.VMEM((2, 64, 128), F32),
            pltpu.VMEM((COUNT, 2, 64, 256), F32),
            pltpu.SemaphoreType.DMA((3,)),
            pltpu.SemaphoreType.DMA((COUNT,)),
            pltpu.SemaphoreType.DMA((COUNT, 1)),
            pltpu.SemaphoreType.DMA((COUNT,)),
        ],
        28,
    )


def right_kernel(count, core_ref, mine, other, err, masked_own, masked_other, *refs):
    hidden = refs[:count]
    keep, away, gram, v_left, v_err, v_hid = refs[count : count + 6]
    v_masked, v_keep, v_away, v_gram, sems, sem_left, sem_err, sem_hid = refs[count + 6 :]
    places = [core_ref[0] * HALF + j if j < HALF else (1 - core_ref[0]) * HALF + j - HALF for j in range(COUNT)]
    loads = list(
        zip(
            factor_loads(mine, other, v_left, sem_left, places),
            error_loads(err, v_err, sem_err, places),
            hidden_loads(hidden, v_hid, sem_hid, places),
        )
    )
    late = [
        pltpu.make_async_copy(masked_own, v_masked.at[pl.ds(0, 128), :], sems.at[0]),
        pltpu.make_async_copy(masked_other, v_masked.at[pl.ds(128, 128), :], sems.at[4]),
    ]
    for j in range(AHEAD):
        start(loads[j])
    start(late)
    w_sum, g_sum, z_sum = 0.0, 0.0, 0.0
    for j in range(COUNT):
        wait(loads[j])
        if j + AHEAD < COUNT:
            start(loads[j + AHEAD])
        terms = stack3(jnp.concatenate([v_left[places[j], 0], v_left[places[j], 1]], axis=1))
        w_sum = w_sum + dot(terms, v_err[places[j]], (1, 0))
        g_sum = g_sum + dot(terms, terms, (1, 1))
        z_sum = z_sum + dot(terms, v_hid[places[j]], (1, 1))
    wait(late)
    z = sum3(z_sum) * (1.0 / 16.0)
    right = sum3(w_sum + dot(stack3(z), v_masked[...], (1, 0)))
    first = core_ref[0] == 0
    v_keep[...] = jnp.where(first, right[:32], right[32:])
    v_away[...] = jnp.where(first, right[32:], right[:32])
    g = sum3(g_sum)
    v_gram[...] = g[:, :64] + g[:, 64:128] + g[:, 128:192]
    stores = [
        pltpu.make_async_copy(v_away, away, sems.at[1]),
        pltpu.make_async_copy(v_keep, keep, sems.at[2]),
        pltpu.make_async_copy(v_gram, gram, sems.at[3]),
    ]
    start(stores)
    wait(stores)


def right_part(core, mine, other, err, hidden, masked_own, masked_other):
    return call(
        functools.partial(right_kernel, len(hidden)),
        "right_part",
        (core, mine, other, err, masked_own, masked_other, *hidden),
        [((32, 512), F32), ((32, 512), F32), ((64, 64), F32)],
        [
            pltpu.VMEM((COUNT, 2, 64, 256), F32),
            pltpu.VMEM((COUNT, BLK, 512), BF),
            pltpu.VMEM((COUNT, 256, BLK), BF),
            pltpu.VMEM((256, 512), BF),
            pltpu.VMEM((32, 512), F32),
            pltpu.VMEM((32, 512), F32),
            pltpu.VMEM((64, 64), F32),
            pltpu.SemaphoreType.DMA((5,)),
            pltpu.SemaphoreType.DMA((COUNT,)),
            pltpu.SemaphoreType.DMA((COUNT,)),
            pltpu.SemaphoreType.DMA((COUNT, len(hidden))),
        ],
        28,
        loose=(9,),
    )


def inverse_kernel(gram, inverse):
    both = jnp.concatenate([gram[...], jnp.eye(64, dtype=F32)], axis=1)
    rows = lax.broadcasted_iota(jnp.int32, (64, 1), 0)
    scale = jnp.zeros((64, 1), F32)
    for j in range(64):
        pivot = both[j : j + 1, j : j + 1]
        scale = jnp.where(rows == j, pivot, scale)
        factor = jnp.where(rows > j, both[:, j : j + 1], 0.0) / pivot
        both = both - factor * both[j : j + 1, :]
    inverse[...] = both[:, 64:] / jnp.sqrt(scale)


def inverse_part(gram):
    return pl.pallas_call(
        inverse_kernel,
        out_shape=jax.ShapeDtypeStruct((64, 64), F32),
        cost_estimate=pl.CostEstimate(flops=1024, bytes_accessed=1024, transcendentals=0),
        name="inverse_part",
    )(gram)


def final_kernel(
    count, core_ref, masked_own, masked_other, total, total_other, inverse, grad_far, grad_base, mine, other, err, *refs
):
    hidden, refs = refs[:count], refs[count:]
    update, new_error, factor, grad = refs[:4]
    v_left, v_err, v_hid, v_masked, v_right, v_inv, v_factor, v_update, v_new, v_grad = refs[4:14]
    sems, sem_left, sem_err, sem_hid, sem_out = refs[14:]
    core = core_ref[0]
    places = [core * HALF + j if j < HALF else (1 - core) * HALF + j - HALF for j in range(COUNT)]
    loads = list(
        zip(
            factor_loads(mine, other, v_left, sem_left, places),
            error_loads(err, v_err, sem_err, places),
            hidden_loads(hidden, v_hid, sem_hid, places),
        )
    )
    small = [
        pltpu.make_async_copy(inverse, v_inv, sems.at[0]),
        pltpu.make_async_copy(total, v_right.at[pl.ds(pl.multiple_of(core * 32, 32), 32), :], sems.at[1]),
        pltpu.make_async_copy(total_other, v_right.at[pl.ds(pl.multiple_of((1 - core) * 32, 32), 32), :], sems.at[2]),
        pltpu.make_async_copy(masked_own, v_masked.at[pl.ds(0, 128), :], sems.at[3]),
        pltpu.make_async_copy(masked_other, v_masked.at[pl.ds(128, 128), :], sems.at[7]),
    ]
    grad_in = pltpu.make_async_copy(grad_far, v_grad, sems.at[4])
    start(small)
    for j in range(AHEAD):
        start(loads[j])
    wait(small)
    v_factor[...] = jnp.dot(v_inv[...], v_right[...], precision=HIGHEST, preferred_element_type=F32) * (1.0 / 64.0)
    coefficients = lax.dot_general(
        v_inv[...], v_factor[...], (((0,), (0,)), ((), ())), precision=HIGHEST, preferred_element_type=F32
    )
    y1, y2, _ = kernel_split3(coefficients)
    ys = jnp.concatenate([y1, y1, y2, y2], axis=0)
    stores = [pltpu.make_async_copy(v_factor, factor, sems.at[5])]
    stores[0].start()
    for j in range(COUNT):
        place = places[j]
        wait(loads[j])
        if j + AHEAD < COUNT:
            start(loads[j + AHEAD])
        elif j + AHEAD == COUNT:
            grad_in.start()
        l1, l2, _ = kernel_split3(jnp.concatenate([v_left[place, 0], v_left[place, 1]], axis=1))
        estimate = dot(jnp.concatenate([l1, l2, l1, l2], axis=0), ys, (0, 0))
        merged = dot(v_hid[place], v_masked[...], (0, 0)) * (1.0 / 16.0) + v_err[place].astype(F32)
        slot = j % SLOTS
        if j >= SLOTS:
            wait(stores[2 * (j - SLOTS) + 1 : 2 * (j - SLOTS) + 3])
        v_update[slot] = estimate.astype(BF)
        v_new[slot] = (merged - estimate).astype(BF)
        for k, (source, target) in enumerate(((v_update, update), (v_new, new_error))):
            copy = pltpu.make_async_copy(source.at[slot], target.at[rows_of(place), :], sem_out.at[k, slot])
            copy.start()
            stores.append(copy)
    grad_in.wait()
    columns = pl.ds(pl.multiple_of((1 - core) * 4096, 4096), 4096)
    stores.append(pltpu.make_async_copy(v_grad, grad.at[:, columns], sems.at[6]))
    stores[-1].start()
    wait(stores[:1] + stores[2 * (COUNT - SLOTS) + 1 :])


def final_part(core, masked_own, masked_other, total, total_other, inverse, grad_far, grad_base, mine, other, err, hidden):
    return call(
        functools.partial(final_kernel, len(hidden)),
        "final_part",
        (core, masked_own, masked_other, total, total_other, inverse, grad_far, grad_base, mine, other, err, *hidden),
        [((8192, 512), BF), ((8192, 512), BF), ((64, 512), F32), ((128, 8192), BF)],
        [
            pltpu.VMEM((COUNT, 2, 64, 256), F32),
            pltpu.VMEM((COUNT, BLK, 512), BF),
            pltpu.VMEM((COUNT, 256, BLK), BF),
            pltpu.VMEM((256, 512), BF),
            pltpu.VMEM((64, 512), F32),
            pltpu.VMEM((64, 64), F32),
            pltpu.VMEM((64, 512), F32),
            pltpu.VMEM((SLOTS, BLK, 512), BF),
            pltpu.VMEM((SLOTS, BLK, 512), BF),
            pltpu.VMEM((128, 4096), BF),
            pltpu.SemaphoreType.DMA((8,)),
            pltpu.SemaphoreType.DMA((COUNT,)),
            pltpu.SemaphoreType.DMA((COUNT,)),
            pltpu.SemaphoreType.DMA((COUNT, len(hidden))),
            pltpu.SemaphoreType.DMA((2, SLOTS)),
        ],
        44,
        aliases={7: 3},
        loose=(3, 4, 5, 6, 14),
    )


def input_kernel(count, core_ref, near_own, near_other, far_own, far_other, key_weight, *refs):
    pieces = refs[:count]
    grad, grad_other, v_near, v_far, v_wnear, v_wfar, v_own, v_other, sems, sem_near, sem_far, sem_out = refs[count:]
    core = core_ref[0]
    small = [
        pltpu.make_async_copy(near_own, v_near.at[pl.ds(0, 128), :], sems.at[0]),
        pltpu.make_async_copy(near_other, v_near.at[pl.ds(128, 128), :], sems.at[1]),
        pltpu.make_async_copy(far_own, v_far.at[pl.ds(0, 128), :], sems.at[2]),
        pltpu.make_async_copy(far_other, v_far.at[pl.ds(128, 128), :], sems.at[3]),
    ]
    loads, fars, ends, row = [], [], [], 0
    for j in range(4):
        place = pl.ds(pl.multiple_of(core * 4096 + j * 1024, 1024), 1024)
        loads.append(pltpu.make_async_copy(key_weight.at[place, :], v_wnear.at[j], sem_near.at[j]))
    for number, piece in enumerate(pieces):
        size = piece.shape[0]
        fars.append(pltpu.make_async_copy(piece, v_wfar.at[pl.ds(row, size), :], sem_far.at[number]))
        row += size
        ends.append(row)
    start(small)
    begun = 0
    for j in range(4):
        loads[j].start()
        while begun < count and (0 if begun == 0 else ends[begun - 1]) < (j + 1) * 1024:
            fars[begun].start()
            begun += 1
    wait(small)
    stores, waited = [], 0
    for j in range(4):
        loads[j].wait()
        while waited < count and (0 if waited == 0 else ends[waited - 1]) < (j + 1) * 1024:
            fars[waited].wait()
            waited += 1
        value = dot(v_near[...], v_wnear[j], (1, 1))
        value = (value + dot(v_far[...], v_wfar[pl.ds(j * 1024, 1024), :], (1, 1))).astype(BF)
        v_own[j] = value[:128]
        v_other[j] = value[128:]
        place = pl.ds(pl.multiple_of(core * 4096 + j * 1024, 1024), 1024)
        stores.append(pltpu.make_async_copy(v_own.at[j], grad.at[:, place], sem_out.at[0, j]))
        stores.append(pltpu.make_async_copy(v_other.at[j], grad_other.at[:, pl.ds(j * 1024, 1024)], sem_out.at[1, j]))
        start(stores[-2:])
    wait(stores)


def input_part(core, near_own, near_other, far_own, far_other, key_weight, pieces):
    return call(
        functools.partial(input_kernel, len(pieces)),
        "input_part",
        (core, near_own, near_other, far_own, far_other, key_weight, *pieces),
        [((128, 8192), BF), ((128, 4096), BF)],
        [
            pltpu.VMEM((256, 512), BF),
            pltpu.VMEM((256, 512), BF),
            pltpu.VMEM((4, 1024, 512), BF),
            pltpu.VMEM((4096, 512), BF),
            pltpu.VMEM((4, 128, 1024), BF),
            pltpu.VMEM((4, 128, 1024), BF),
            pltpu.SemaphoreType.DMA((4,)),
            pltpu.SemaphoreType.DMA((4,)),
            pltpu.SemaphoreType.DMA((len(pieces),)),
            pltpu.SemaphoreType.DMA((2, 4)),
        ],
        18,
    )


def local(hidden_rows, key_grads, loss_mask, key_weight, error_buf, right_factor):
    core = lax.axis_index("core")
    core_arg = core.astype(jnp.int32)[None]
    xl_arg = lax.axis_index("xl").astype(jnp.int32)[None]
    err = error_buf.reshape(8192, 512)
    barrier = lax.optimization_barrier

    def weight_rows(first, rows):
        return lax.dynamic_slice(key_weight, (core * 4096 + first, 0), (rows, 512))

    masked_own, masked_other, tok_own, tok_other, terms_t = token_part(
        xl_arg, key_grads, loss_mask.reshape(1, 256), right_factor.T
    )

    tok_far = send(tok_other, PARTNER)

    lots = [("hidden", 0, 32), ("hidden", 32, 64), ("hidden", 96, 32)]
    first = 0
    for rows in (512, 1024, 512, 1024, 1024):
        lots.append(("weight", first, rows))
        first += rows
    parcels = parcel_part(core_arg, masked_own, hidden_rows, key_weight, lots)
    parcels, weights = list(parcels[:3]), list(parcels[3:])
    tok_far, parcels[0], weights[0] = barrier((tok_far, parcels[0], weights[0]))
    far_hidden = [send(parcels[0], PARTNER)]
    far_weight = [send(weights[0], WRAP)]

    keep, away = left_part(core_arg, err, hidden_rows, terms_t, tok_own, tok_far)
    keep, away, far_hidden[0], far_weight[0], parcels[1], weights[1] = barrier(
        (keep, away, far_hidden[0], far_weight[0], parcels[1], weights[1])
    )
    piece = keep + send(away, OTHER_CORE)
    far_hidden.append(send(parcels[1], PARTNER))
    far_weight.append(send(weights[1], WRAP))
    far_hidden[1], far_weight[1], masked_own = barrier((far_hidden[1], far_weight[1], masked_own))
    near_other = send(masked_own, OTHER_CORE)
    piece = lax.all_to_all(piece, ("z", "y"), 0, 0, tiled=True)
    piece = jnp.sum(piece, axis=0)
    piece, near_other = barrier((piece, near_other))
    piece = sum_of_four(piece, "x")

    piece, parcels[2], weights[2], weights[3], weights[4], masked_other = barrier(
        (piece, parcels[2], weights[2], weights[3], weights[4], masked_other)
    )
    masked_far = send(masked_other, PARTNER)
    far_hidden.append(send(parcels[2], PARTNER))
    far_weight.append(send(weights[2], WRAP))
    mine = lax.all_to_all(jnp.broadcast_to(piece[None], (16, 64, 256)), ("z", "y"), 0, 0, tiled=True)
    mine, far_hidden[2], far_weight[2], masked_far = barrier((mine, far_hidden[2], far_weight[2], masked_far))
    far_weight.append(send(weights[3], WRAP))
    far_weight.append(send(weights[4], PARTNER))
    far_other = send(masked_far, OTHER_CORE)
    other = send(mine, OTHER_CORE)
    other, far_other = barrier((other, far_other))

    hidden = [hidden_rows, *far_hidden]
    keep, away, gram = right_part(core_arg, mine, other, err, hidden, masked_own, masked_other)
    total = keep + send(away, OTHER_CORE)
    total, gram = barrier((total, gram))
    inverse = inverse_part(gram)
    total = sum_of_four(total, "y")
    total, inverse, far_weight[3], far_weight[4] = barrier((total, inverse, far_weight[3], far_weight[4]))
    grad, grad_other = input_part(core_arg, masked_own, near_other, masked_far, far_other, key_weight, far_weight)
    total = sum_of_four(total, "z")
    total, grad_other = barrier((total, grad_other))
    grad_far = send(grad_other, OTHER_CORE)
    total = total + send(total, permutation(x=2))
    total_other = send(total, OTHER_CORE)

    update, new_error, factor, input_grad = final_part(
        core_arg, masked_own, masked_other, total, total_other, inverse, grad_far, grad, mine, other, err, hidden
    )
    return input_grad, update, new_error[None], factor.T


def solution(mesh):
    fine = Mesh(mesh.devices.reshape(SIZES), AXES)
    dp = ("z", "y", "xh", "core")
    placed = (
        P(AXES, None),
        P(dp, "xl"),
        P(dp),
        P(None, "xl"),
        P(dp, None, "xl"),
        P("xl", None),
    )
    return jax.shard_map(
        local,
        mesh=fine,
        in_specs=placed,
        out_specs=(P(AXES, None), P(None, "xl"), P(dp, None, "xl"), P("xl", None)),
        check_vma=False,
    )
```

```python
import functools

import jax
import jax.numpy as jnp
import numpy as np
from jax import lax
from jax.experimental import pallas as pl
from jax.experimental.pallas import tpu as pltpu
from jax.sharding import Mesh
from jax.sharding import PartitionSpec as P

AXES = ("z", "y", "xh", "core", "xl")
SIZES = (4, 4, 2, 2, 2)
BF = jnp.bfloat16
F32 = jnp.float32
HIGHEST = lax.Precision.HIGHEST
BLK = 512
AHEAD = 4
SLOTS = 16
COUNT = 8192 // BLK
HALF = COUNT // 2


def permutation(z=0, y=0, x=0, core=0, pairs=None):
    result = []
    for source in range(128):
        cz, cy, ch, cc, cl = (int(v) for v in np.unravel_index(source, SIZES))
        place = {"z": cz, "y": cy, "x": ch * 2 + cl}
        if pairs is not None:
            place[pairs[0]] = ((1, 0, 3, 2), (3, 2, 1, 0))[pairs[1]][place[pairs[0]]]
        cz, cy, cx = (place["z"] + z) % 4, (place["y"] + y) % 4, (place["x"] + x) % 4
        target = (cz, cy, cx // 2, (cc + core) % 2, cx % 2)
        result.append((source, int(np.ravel_multi_index(target, SIZES))))
    return result


OTHER_CORE = permutation(core=1)
PARTNER = permutation(pairs=("x", 0))
WRAP = permutation(pairs=("x", 1))


def send(array, pairs):
    return lax.ppermute(array, AXES, pairs)


def sum_of_four(array, axis):
    ahead = send(array, permutation(**{axis: 1}))
    behind = send(array, permutation(**{axis: 3}))
    across = send(array, permutation(**{axis: 2}))
    return (array + across) + (ahead + behind)


def kernel_split3(value):
    a = value.astype(BF)
    rest = value - a.astype(F32)
    b = rest.astype(BF)
    c = (rest - b.astype(F32)).astype(BF)
    return a, b, c


def stack3(value):
    return jnp.concatenate(kernel_split3(value), axis=0)


def sum3(value):
    return value[:64] + value[64:128] + value[128:192]


def dot(a, b, contract):
    return lax.dot_general(a, b, ((contract[:1], contract[1:]), ((), ())), preferred_element_type=F32)


def start(copies):
    for copy in copies:
        copy.start()


def wait(copies):
    for copy in copies:
        copy.wait()


def call(kernel, name, operands, outs, scratch, limit, aliases=None, hbm=False, loose=()):
    anywhere = pl.BlockSpec(memory_space=pl.ANY)
    far = [
        array if number in loose else pltpu.with_memory_space_constraint(array, pltpu.HBM)
        for number, array in enumerate(operands[1:], 1)
    ]
    return pl.pallas_call(
        kernel,
        out_shape=[(pltpu.HBM if hbm else jax.ShapeDtypeStruct)(shape, dtype) for shape, dtype in outs],
        in_specs=[pl.BlockSpec(memory_space=pltpu.SMEM)] + [anywhere if n in loose else pl.BlockSpec(memory_space=pltpu.HBM) for n in range(1, len(operands))],
        out_specs=[anywhere] * len(outs),
        scratch_shapes=scratch,
        input_output_aliases=aliases or {},
        compiler_params=pltpu.CompilerParams(vmem_limit_bytes=limit * 2**20),
        cost_estimate=pl.CostEstimate(flops=1024, bytes_accessed=1024, transcendentals=0),
        name=name,
    )(operands[0], *far)


def rows_of(block):
    return pl.ds(pl.multiple_of(block * BLK, BLK), BLK)


def error_loads(err, v_err, sems, places):
    return [pltpu.make_async_copy(err.at[rows_of(p), :], v_err.at[p], sems.at[j]) for j, p in enumerate(places)]


class Group:
    def __init__(self, copies):
        self.copies = copies

    def start(self):
        start(self.copies)

    def wait(self):
        wait(self.copies)


def hidden_loads(hidden, v_hid, sems, places):
    groups = []
    for j, place in enumerate(places):
        copies, row = [], 0
        for number, part in enumerate(hidden):
            size = part.shape[0]
            copies.append(
                pltpu.make_async_copy(part.at[:, rows_of(place)], v_hid.at[place, pl.ds(row, size), :], sems.at[j, number])
            )
            row += size
        groups.append(Group(copies))
    return groups


def factor_loads(mine, other, v_left, sems, places):
    return [
        pltpu.make_async_copy((mine, other)[j // HALF].at[pl.ds(2 * (j % HALF), 2)], v_left.at[p], sems.at[j])
        for j, p in enumerate(places)
    ]


def token_kernel(
    xl_ref, grads, mask, factor_t, own, other, tok_own, tok_other, terms_t, v_grads, v_mask, v_factor, v_tok, v_masked, v_terms, sems
):
    loads = [
        pltpu.make_async_copy(grads, v_grads, sems.at[0]),
        pltpu.make_async_copy(mask, v_mask, sems.at[1]),
        pltpu.make_async_copy(factor_t, v_factor, sems.at[2]),
    ]
    start(loads)
    wait(loads)
    flags = jnp.broadcast_to(v_mask[...].astype(F32), (128, 256)).T[:, :1]
    masked = (v_grads[...].astype(F32) * flags).astype(BF)
    terms = stack3(v_factor[...])
    tok = sum3(dot(terms, masked, (1, 1))) * (1.0 / 16.0)
    first = xl_ref[0] == 0
    v_tok[0] = jnp.where(first, tok[:, 128:], tok[:, :128])
    v_tok[1] = jnp.where(first, tok[:, :128], tok[:, 128:])
    v_terms[...] = terms
    v_masked[0] = jnp.where(first, masked[:128], masked[128:])
    v_masked[1] = jnp.where(first, masked[128:], masked[:128])
    stores = [
        pltpu.make_async_copy(v_tok.at[0], tok_other, sems.at[3]),
        pltpu.make_async_copy(v_tok.at[1], tok_own, sems.at[4]),
        pltpu.make_async_copy(v_terms, terms_t, sems.at[5]),
        pltpu.make_async_copy(v_masked.at[0], own, sems.at[6]),
        pltpu.make_async_copy(v_masked.at[1], other, sems.at[7]),
    ]
    start(stores)
    wait(stores)


def token_part(xl, grads, mask, factor_t):
    return call(
        token_kernel,
        "token_part",
        (xl, grads, mask, factor_t),
        [((128, 512), BF), ((128, 512), BF), ((64, 128), F32), ((64, 128), F32), ((192, 512), BF)],
        [
            pltpu.VMEM((256, 512), BF),
            pltpu.VMEM((1, 256), jnp.int32),
            pltpu.VMEM((64, 512), F32),
            pltpu.VMEM((2, 64, 128), F32),
            pltpu.VMEM((2, 128, 512), BF),
            pltpu.VMEM((192, 512), BF),
            pltpu.SemaphoreType.DMA((8,)),
        ],
        8,
        hbm=True,
    )


def parcel_kernel(firsts, core_ref, after, hidden, key_weight, *refs):
    count = len(firsts)
    parcels, v_parcels, sems = refs[:count], refs[count : 2 * count], refs[2 * count]
    picks, drops = [], []
    for k, (kind, first) in enumerate(firsts):
        rows = parcels[k].shape[0]
        if kind == "hidden":
            source = hidden.at[pl.ds(first, rows), :]
        else:
            source = key_weight.at[pl.ds(pl.multiple_of(core_ref[0] * 4096 + first, 32), rows), :]
        picks.append(pltpu.make_async_copy(source, v_parcels[k], sems.at[0, k]))
        drops.append(pltpu.make_async_copy(v_parcels[k], parcels[k], sems.at[1, k]))
    start(picks)
    for pick, drop in zip(picks, drops):
        pick.wait()
        drop.start()
    wait(drops)


def parcel_part(core, after, hidden, key_weight, parcels):
    shapes = [((rows, 8192 if kind == "hidden" else 512), BF) for kind, _, rows in parcels]
    return call(
        functools.partial(parcel_kernel, [(kind, first) for kind, first, _ in parcels]),
        "parcel_part",
        (core, after, hidden, key_weight),
        shapes,
        [*[pltpu.VMEM(shape, dtype) for shape, dtype in shapes], pltpu.SemaphoreType.DMA((2, len(shapes)))],
        10,
        hbm=True,
    )


def left_kernel(
    core_ref, err, hidden, terms_t, tok_own, tok_far, keep, away, v_err, v_hid, v_terms, v_tok, v_out, sems, sem_err, sem_hid, sem_out
):
    small = [
        pltpu.make_async_copy(terms_t, v_terms, sems.at[0]),
        pltpu.make_async_copy(tok_own, v_tok.at[0], sems.at[1]),
        pltpu.make_async_copy(tok_far, v_tok.at[1], sems.at[2]),
    ]
    places = [(1 - core_ref[0]) * HALF + j if j < HALF else core_ref[0] * HALF + j - HALF for j in range(COUNT)]
    loads = list(zip(error_loads(err, v_err, sem_err, places), hidden_loads([hidden], v_hid, sem_hid, places)))
    start(small)
    for j in range(AHEAD):
        start(loads[j])
    wait(small)
    toks = stack3(v_tok[0] + v_tok[1])
    stores = []
    for j in range(COUNT):
        wait(loads[j])
        if j + AHEAD < COUNT:
            start(loads[j + AHEAD])
        value = sum3(dot(v_terms[...], v_err[places[j]], (1, 1)) + dot(toks, v_hid[places[j]], (1, 0)))
        v_out[j, 0] = value[:, :256]
        v_out[j, 1] = value[:, 256:]
        target = away if j < HALF else keep
        stores.append(pltpu.make_async_copy(v_out.at[j], target.at[pl.ds(2 * (j % HALF), 2)], sem_out.at[j]))
        stores[j].start()
    wait(stores)


def left_part(core, err, hidden, terms_t, tok_own, tok_far):
    return call(
        left_kernel,
        "left_part",
        (core, err, hidden, terms_t, tok_own, tok_far),
        [((16, 64, 256), F32), ((16, 64, 256), F32)],
        [
            pltpu.VMEM((COUNT, BLK, 512), BF),
            pltpu.VMEM((COUNT, 128, BLK), BF),
            pltpu.VMEM((192, 512), BF),
            pltpu.VMEM((2, 64, 128), F32),
            pltpu.VMEM((COUNT, 2, 64, 256), F32),
            pltpu.SemaphoreType.DMA((3,)),
            pltpu.SemaphoreType.DMA((COUNT,)),
            pltpu.SemaphoreType.DMA((COUNT, 1)),
            pltpu.SemaphoreType.DMA((COUNT,)),
        ],
        28,
    )


def right_kernel(count, core_ref, mine, other, err, masked_own, masked_other, *refs):
    hidden = refs[:count]
    keep, away, gram, v_left, v_err, v_hid = refs[count : count + 6]
    v_masked, v_keep, v_away, v_gram, sems, sem_left, sem_err, sem_hid = refs[count + 6 :]
    places = [core_ref[0] * HALF + j if j < HALF else (1 - core_ref[0]) * HALF + j - HALF for j in range(COUNT)]
    loads = list(
        zip(
            factor_loads(mine, other, v_left, sem_left, places),
            error_loads(err, v_err, sem_err, places),
            hidden_loads(hidden, v_hid, sem_hid, places),
        )
    )
    late = [
        pltpu.make_async_copy(masked_own, v_masked.at[pl.ds(0, 128), :], sems.at[0]),
        pltpu.make_async_copy(masked_other, v_masked.at[pl.ds(128, 128), :], sems.at[4]),
    ]
    for j in range(AHEAD):
        start(loads[j])
    start(late)
    w_sum, g_sum, z_sum = 0.0, 0.0, 0.0
    for j in range(COUNT):
        wait(loads[j])
        if j + AHEAD < COUNT:
            start(loads[j + AHEAD])
        terms = stack3(jnp.concatenate([v_left[places[j], 0], v_left[places[j], 1]], axis=1))
        w_sum = w_sum + dot(terms, v_err[places[j]], (1, 0))
        g_sum = g_sum + dot(terms, terms, (1, 1))
        z_sum = z_sum + dot(terms, v_hid[places[j]], (1, 1))
    wait(late)
    z = sum3(z_sum) * (1.0 / 16.0)
    right = sum3(w_sum + dot(stack3(z), v_masked[...], (1, 0)))
    first = core_ref[0] == 0
    v_keep[...] = jnp.where(first, right[:32], right[32:])
    v_away[...] = jnp.where(first, right[32:], right[:32])
    g = sum3(g_sum)
    v_gram[...] = g[:, :64] + g[:, 64:128] + g[:, 128:192]
    stores = [
        pltpu.make_async_copy(v_away, away, sems.at[1]),
        pltpu.make_async_copy(v_keep, keep, sems.at[2]),
        pltpu.make_async_copy(v_gram, gram, sems.at[3]),
    ]
    start(stores)
    wait(stores)


def right_part(core, mine, other, err, hidden, masked_own, masked_other):
    return call(
        functools.partial(right_kernel, len(hidden)),
        "right_part",
        (core, mine, other, err, masked_own, masked_other, *hidden),
        [((32, 512), F32), ((32, 512), F32), ((64, 64), F32)],
        [
            pltpu.VMEM((COUNT, 2, 64, 256), F32),
            pltpu.VMEM((COUNT, BLK, 512), BF),
            pltpu.VMEM((COUNT, 256, BLK), BF),
            pltpu.VMEM((256, 512), BF),
            pltpu.VMEM((32, 512), F32),
            pltpu.VMEM((32, 512), F32),
            pltpu.VMEM((64, 64), F32),
            pltpu.SemaphoreType.DMA((5,)),
            pltpu.SemaphoreType.DMA((COUNT,)),
            pltpu.SemaphoreType.DMA((COUNT,)),
            pltpu.SemaphoreType.DMA((COUNT, len(hidden))),
        ],
        28,
        loose=(9,),
    )


def inverse_kernel(gram, inverse):
    both = jnp.concatenate([gram[...], jnp.eye(64, dtype=F32)], axis=1)
    rows = lax.broadcasted_iota(jnp.int32, (64, 1), 0)
    scale = jnp.zeros((64, 1), F32)
    for j in range(64):
        pivot = both[j : j + 1, j : j + 1]
        scale = jnp.where(rows == j, pivot, scale)
        factor = jnp.where(rows > j, both[:, j : j + 1], 0.0) / pivot
        both = both - factor * both[j : j + 1, :]
    inverse[...] = both[:, 64:] / jnp.sqrt(scale)


def inverse_part(gram):
    return pl.pallas_call(
        inverse_kernel,
        out_shape=jax.ShapeDtypeStruct((64, 64), F32),
        cost_estimate=pl.CostEstimate(flops=1024, bytes_accessed=1024, transcendentals=0),
        name="inverse_part",
    )(gram)


def final_kernel(
    count, core_ref, masked_own, masked_other, total, total_other, inverse, grad_far, grad_base, mine, other, err, *refs
):
    hidden, refs = refs[:count], refs[count:]
    update, new_error, factor, grad = refs[:4]
    v_left, v_err, v_hid, v_masked, v_right, v_inv, v_factor, v_update, v_new, v_grad = refs[4:14]
    sems, sem_left, sem_err, sem_hid, sem_out = refs[14:]
    core = core_ref[0]
    places = [core * HALF + j if j < HALF else (1 - core) * HALF + j - HALF for j in range(COUNT)]
    loads = list(
        zip(
            factor_loads(mine, other, v_left, sem_left, places),
            error_loads(err, v_err, sem_err, places),
            hidden_loads(hidden, v_hid, sem_hid, places),
        )
    )
    small = [
        pltpu.make_async_copy(inverse, v_inv, sems.at[0]),
        pltpu.make_async_copy(total, v_right.at[pl.ds(pl.multiple_of(core * 32, 32), 32), :], sems.at[1]),
        pltpu.make_async_copy(total_other, v_right.at[pl.ds(pl.multiple_of((1 - core) * 32, 32), 32), :], sems.at[2]),
        pltpu.make_async_copy(masked_own, v_masked.at[pl.ds(0, 128), :], sems.at[3]),
        pltpu.make_async_copy(masked_other, v_masked.at[pl.ds(128, 128), :], sems.at[7]),
    ]
    grad_in = pltpu.make_async_copy(grad_far, v_grad, sems.at[4])
    start(small)
    for j in range(AHEAD):
        start(loads[j])
    wait(small)
    v_factor[...] = jnp.dot(v_inv[...], v_right[...], precision=HIGHEST, preferred_element_type=F32) * (1.0 / 64.0)
    coefficients = lax.dot_general(
        v_inv[...], v_factor[...], (((0,), (0,)), ((), ())), precision=HIGHEST, preferred_element_type=F32
    )
    y1, y2, _ = kernel_split3(coefficients)
    ys = jnp.concatenate([y1, y1, y2, y2], axis=0)
    stores = [pltpu.make_async_copy(v_factor, factor, sems.at[5])]
    stores[0].start()
    for j in range(COUNT):
        place = places[j]
        wait(loads[j])
        if j + AHEAD < COUNT:
            start(loads[j + AHEAD])
        elif j + AHEAD == COUNT:
            grad_in.start()
        l1, l2, _ = kernel_split3(jnp.concatenate([v_left[place, 0], v_left[place, 1]], axis=1))
        estimate = dot(jnp.concatenate([l1, l2, l1, l2], axis=0), ys, (0, 0))
        merged = dot(v_hid[place], v_masked[...], (0, 0)) * (1.0 / 16.0) + v_err[place].astype(F32)
        slot = j % SLOTS
        if j >= SLOTS:
            wait(stores[2 * (j - SLOTS) + 1 : 2 * (j - SLOTS) + 3])
        v_update[slot] = estimate.astype(BF)
        v_new[slot] = (merged - estimate).astype(BF)
        for k, (source, target) in enumerate(((v_update, update), (v_new, new_error))):
            copy = pltpu.make_async_copy(source.at[slot], target.at[rows_of(place), :], sem_out.at[k, slot])
            copy.start()
            stores.append(copy)
    grad_in.wait()
    columns = pl.ds(pl.multiple_of((1 - core) * 4096, 4096), 4096)
    stores.append(pltpu.make_async_copy(v_grad, grad.at[:, columns], sems.at[6]))
    stores[-1].start()
    wait(stores[:1] + stores[2 * (COUNT - SLOTS) + 1 :])


def final_part(core, masked_own, masked_other, total, total_other, inverse, grad_far, grad_base, mine, other, err, hidden):
    return call(
        functools.partial(final_kernel, len(hidden)),
        "final_part",
        (core, masked_own, masked_other, total, total_other, inverse, grad_far, grad_base, mine, other, err, *hidden),
        [((8192, 512), BF), ((8192, 512), BF), ((64, 512), F32), ((128, 8192), BF)],
        [
            pltpu.VMEM((COUNT, 2, 64, 256), F32),
            pltpu.VMEM((COUNT, BLK, 512), BF),
            pltpu.VMEM((COUNT, 256, BLK), BF),
            pltpu.VMEM((256, 512), BF),
            pltpu.VMEM((64, 512), F32),
            pltpu.VMEM((64, 64), F32),
            pltpu.VMEM((64, 512), F32),
            pltpu.VMEM((SLOTS, BLK, 512), BF),
            pltpu.VMEM((SLOTS, BLK, 512), BF),
            pltpu.VMEM((128, 4096), BF),
            pltpu.SemaphoreType.DMA((8,)),
            pltpu.SemaphoreType.DMA((COUNT,)),
            pltpu.SemaphoreType.DMA((COUNT,)),
            pltpu.SemaphoreType.DMA((COUNT, len(hidden))),
            pltpu.SemaphoreType.DMA((2, SLOTS)),
        ],
        44,
        aliases={7: 3},
        loose=(3, 4, 5, 6, 14),
    )


def input_kernel(count, core_ref, near_own, near_other, far_own, far_other, key_weight, *refs):
    pieces = refs[:count]
    grad, grad_other, v_near, v_far, v_wnear, v_wfar, v_own, v_other, sems, sem_near, sem_far, sem_out = refs[count:]
    core = core_ref[0]
    small = [
        pltpu.make_async_copy(near_own, v_near.at[pl.ds(0, 128), :], sems.at[0]),
        pltpu.make_async_copy(near_other, v_near.at[pl.ds(128, 128), :], sems.at[1]),
        pltpu.make_async_copy(far_own, v_far.at[pl.ds(0, 128), :], sems.at[2]),
        pltpu.make_async_copy(far_other, v_far.at[pl.ds(128, 128), :], sems.at[3]),
    ]
    loads, fars, ends, row = [], [], [], 0
    for j in range(4):
        place = pl.ds(pl.multiple_of(core * 4096 + j * 1024, 1024), 1024)
        loads.append(pltpu.make_async_copy(key_weight.at[place, :], v_wnear.at[j], sem_near.at[j]))
    for number, piece in enumerate(pieces):
        size = piece.shape[0]
        fars.append(pltpu.make_async_copy(piece, v_wfar.at[pl.ds(row, size), :], sem_far.at[number]))
        row += size
        ends.append(row)
    start(small)
    begun = 0
    for j in range(4):
        loads[j].start()
        while begun < count and (0 if begun == 0 else ends[begun - 1]) < (j + 1) * 1024:
            fars[begun].start()
            begun += 1
    wait(small)
    stores, waited = [], 0
    for j in range(4):
        loads[j].wait()
        while waited < count and (0 if waited == 0 else ends[waited - 1]) < (j + 1) * 1024:
            fars[waited].wait()
            waited += 1
        value = dot(v_near[...], v_wnear[j], (1, 1))
        value = (value + dot(v_far[...], v_wfar[pl.ds(j * 1024, 1024), :], (1, 1))).astype(BF)
        v_own[j] = value[:128]
        v_other[j] = value[128:]
        place = pl.ds(pl.multiple_of(core * 4096 + j * 1024, 1024), 1024)
        stores.append(pltpu.make_async_copy(v_own.at[j], grad.at[:, place], sem_out.at[0, j]))
        stores.append(pltpu.make_async_copy(v_other.at[j], grad_other.at[:, pl.ds(j * 1024, 1024)], sem_out.at[1, j]))
        start(stores[-2:])
    wait(stores)


def input_part(core, near_own, near_other, far_own, far_other, key_weight, pieces):
    return call(
        functools.partial(input_kernel, len(pieces)),
        "input_part",
        (core, near_own, near_other, far_own, far_other, key_weight, *pieces),
        [((128, 8192), BF), ((128, 4096), BF)],
        [
            pltpu.VMEM((256, 512), BF),
            pltpu.VMEM((256, 512), BF),
            pltpu.VMEM((4, 1024, 512), BF),
            pltpu.VMEM((4096, 512), BF),
            pltpu.VMEM((4, 128, 1024), BF),
            pltpu.VMEM((4, 128, 1024), BF),
            pltpu.SemaphoreType.DMA((4,)),
            pltpu.SemaphoreType.DMA((4,)),
            pltpu.SemaphoreType.DMA((len(pieces),)),
            pltpu.SemaphoreType.DMA((2, 4)),
        ],
        18,
    )


def local(hidden_rows, key_grads, loss_mask, key_weight, error_buf, right_factor):
    core = lax.axis_index("core")
    core_arg = core.astype(jnp.int32)[None]
    xl_arg = lax.axis_index("xl").astype(jnp.int32)[None]
    err = error_buf.reshape(8192, 512)
    barrier = lax.optimization_barrier

    def weight_rows(first, rows):
        return lax.dynamic_slice(key_weight, (core * 4096 + first, 0), (rows, 512))

    masked_own, masked_other, tok_own, tok_other, terms_t = token_part(
        xl_arg, key_grads, loss_mask.reshape(1, 256), right_factor.T
    )

    tok_far = send(tok_other, PARTNER)

    lots = [("hidden", 0, 32), ("hidden", 32, 64), ("hidden", 96, 32)]
    first = 0
    for rows in (512, 1024, 544, 992, 1024):
        lots.append(("weight", first, rows))
        first += rows
    parcels = parcel_part(core_arg, masked_own, hidden_rows, key_weight, lots)
    parcels, weights = list(parcels[:3]), list(parcels[3:])
    tok_far, parcels[0], weights[0] = barrier((tok_far, parcels[0], weights[0]))
    far_hidden = [send(parcels[0], PARTNER)]
    far_weight = [send(weights[0], WRAP)]

    keep, away = left_part(core_arg, err, hidden_rows, terms_t, tok_own, tok_far)
    keep, away, far_hidden[0], far_weight[0], parcels[1], weights[1] = barrier(
        (keep, away, far_hidden[0], far_weight[0], parcels[1], weights[1])
    )
    piece = keep + send(away, OTHER_CORE)
    far_hidden.append(send(parcels[1], PARTNER))
    far_weight.append(send(weights[1], WRAP))
    far_hidden[1], far_weight[1], masked_own = barrier((far_hidden[1], far_weight[1], masked_own))
    near_other = send(masked_own, OTHER_CORE)
    piece = lax.all_to_all(piece, ("z", "y"), 0, 0, tiled=True)
    piece = jnp.sum(piece, axis=0)
    piece, near_other = barrier((piece, near_other))
    piece = sum_of_four(piece, "x")

    piece, parcels[2], weights[2], weights[3], weights[4], masked_other = barrier(
        (piece, parcels[2], weights[2], weights[3], weights[4], masked_other)
    )
    masked_far = send(masked_other, PARTNER)
    far_hidden.append(send(parcels[2], PARTNER))
    far_weight.append(send(weights[2], WRAP))
    mine = lax.all_to_all(jnp.broadcast_to(piece[None], (16, 64, 256)), ("z", "y"), 0, 0, tiled=True)
    mine, far_hidden[2], far_weight[2], masked_far = barrier((mine, far_hidden[2], far_weight[2], masked_far))
    far_weight.append(send(weights[3], WRAP))
    far_weight.append(send(weights[4], PARTNER))
    far_other = send(masked_far, OTHER_CORE)
    other = send(mine, OTHER_CORE)
    other, far_other = barrier((other, far_other))

    hidden = [hidden_rows, *far_hidden]
    keep, away, gram = right_part(core_arg, mine, other, err, hidden, masked_own, masked_other)
    total = keep + send(away, OTHER_CORE)
    total, gram = barrier((total, gram))
    inverse = inverse_part(gram)
    total = sum_of_four(total, "y")
    total, inverse, far_weight[3], far_weight[4] = barrier((total, inverse, far_weight[3], far_weight[4]))
    grad, grad_other = input_part(core_arg, masked_own, near_other, masked_far, far_other, key_weight, far_weight)
    total = sum_of_four(total, "z")
    total, grad_other = barrier((total, grad_other))
    grad_far = send(grad_other, OTHER_CORE)
    total = total + send(total, permutation(x=2))
    total_other = send(total, OTHER_CORE)

    update, new_error, factor, input_grad = final_part(
        core_arg, masked_own, masked_other, total, total_other, inverse, grad_far, grad, mine, other, err, hidden
    )
    return input_grad, update, new_error[None], factor.T


def solution(mesh):
    fine = Mesh(mesh.devices.reshape(SIZES), AXES)
    dp = ("z", "y", "xh", "core")
    placed = (
        P(AXES, None),
        P(dp, "xl"),
        P(dp),
        P(None, "xl"),
        P(dp, None, "xl"),
        P("xl", None),
    )
    return jax.shard_map(
        local,
        mesh=fine,
        in_specs=placed,
        out_specs=(P(AXES, None), P(None, "xl"), P(dp, None, "xl"), P("xl", None)),
        check_vma=False,
    )
```
